128 devices in a mesh: section: 32 (over y, x, core), tp: 4 (over z).
Axes of the slice: x: 4, y: 4, z: 4, core: 2. Of those that a mesh axis runs over, the one named last changes fastest.
Arguments:
- tokens: bfloat16 [512, 2048], P('tp'), may hold values from -6 to 6
- cotangent: bfloat16 [512, 2048], P('tp'), may hold values from -0.119628906 to 0.119628906
- value_weight: bfloat16 [32, 2048, 512], P('section', None, 'tp'), may hold values from -0.125 to 0.125
- output_weight: bfloat16 [32, 2048, 512], P('section', None, 'tp'), may hold values from -0.25 to 0.25
- value_first: float32 [32, 2048, 512], P('section', None, 'tp'), may hold values from -1.8 to 1.8
- output_first: float32 [32, 2048, 512], P('section', None, 'tp'), may hold values from -1.8 to 1.8
- value_second: float32 [32, 2048, 512], P('section', None, 'tp'), may hold values from 0.01 to 1
- output_second: float32 [32, 2048, 512], P('section', None, 'tp'), may hold values from 0.01 to 1
- layer_map: int32 [24], replicated, may hold values from 0 to 15, as said below
- old_section: int32 [16], replicated, may hold values from 0 to 31, as said below
- new_section: int32 [24], replicated, may hold values from 0 to 31, as said below
Outputs:
- new_value_weight: bfloat16 [32, 2048, 512], P('section', None, 'tp')
- new_output_weight: bfloat16 [32, 2048, 512], P('section', None, 'tp')
- new_value_first: float32 [32, 2048, 512], P('section', None, 'tp')
- new_output_first: float32 [32, 2048, 512], P('section', None, 'tp')
- new_value_second: float32 [32, 2048, 512], P('section', None, 'tp')
- new_output_second: float32 [32, 2048, 512], P('section', None, 'tp')
The draws below stay inside these ranges and needn't reach their ends.
Inputs may be any that keep to these rules, and one draw needn't show every extreme that they name: `layer_map`: Non-decreasing; every old layer appears once or twice. `old_section`: strictly increasing. `new_section`: strictly increasing.
All inputs are finite; a program needn't handle non-finite values.
Results may differ from the reference program's by a relative error of at most 0.025.
Values may be sent and summed in bfloat16 or wider, within the bound.
A program may use at most 128 MiB of HBM per device.

```python
import math
import jax
import jax.numpy as jnp
from jax import lax

D = 2048
KVW = 512
TOKENS = 512
SECTIONS = 32
OLD = 16
NEW = 24


def draw_layer_map(key, part):
    shuffled = jax.random.permutation(jax.random.fold_in(key, 5), OLD)
    doubled = (shuffled < NEW - OLD).astype(jnp.int32)
    bounds = jnp.cumsum(1 + doubled)
    positions = lax.iota(jnp.int32, NEW)
    return jnp.sum((bounds[None, :] <= positions[:, None]).astype(jnp.int32), axis=1).astype(jnp.int32)


def ends_included(key, count):
    shuffled = jax.random.permutation(key, SECTIONS - 2) + 1
    inner = shuffled[:count - 2].astype(jnp.int32)
    first = jnp.zeros((1,), jnp.int32)
    final = jnp.full((1,), SECTIONS - 1, jnp.int32)
    return jnp.sort(jnp.concatenate([first, inner, final])).astype(jnp.int32)


def draw_old_section(key, part):
    return ends_included(jax.random.fold_in(key, 11), OLD)


def draw_new_section(key, part):
    return ends_included(jax.random.fold_in(key, 23), NEW)


def level_of(key, extent, pieces, least, high):
    gain, own = 1.0, jax.random.fold_in(key, 6)
    for dim, shards_of in pieces:
        heights = jnp.exp(jax.random.uniform(jax.random.fold_in(own, dim), (shards_of,), jnp.float32, least / len(pieces), high / len(pieces)))
        gain = gain * jnp.repeat(heights, extent[dim] // shards_of).reshape([-1 if axis == dim else 1 for axis in range(len(extent))])
    return gain


def noise(stream_key, dims, deviation, most, split=(), held_as=jnp.bfloat16):
    entries = deviation * jax.random.normal(stream_key, dims, jnp.float32)
    if split:
        entries = entries * level_of(stream_key, dims, split, -0.22, 0.18)
    return jnp.clip(entries, -most, most).astype(held_as)


def setup_inputs(seed: int = 0) -> dict:
    key_of = jax.random.split(jax.random.key(seed), 12)
    tokens = noise(key_of[0], (TOKENS, D), 1.0, 6.0, ((0, 4),))
    cotangent = noise(key_of[1], (TOKENS, D), 0.02, 0.119628906, ((0, 4),))
    value_weight = noise(key_of[2], (SECTIONS, D, KVW), D ** -0.5, 0.125, ((0, 32), (2, 4)))
    output_weight = noise(key_of[3], (SECTIONS, D, KVW), KVW ** -0.5, 0.25, ((0, 32), (2, 4)))
    value_first = noise(key_of[4], (SECTIONS, D, KVW), 0.3, 1.8, ((0, 32), (2, 4)), jnp.float32)
    output_first = noise(key_of[5], (SECTIONS, D, KVW), 0.3, 1.8, ((0, 32), (2, 4)), jnp.float32)
    value_second = jnp.clip(jnp.exp(math.log(1.0) - 4.6051702 * jax.random.uniform(key_of[6], (SECTIONS, D, KVW), jnp.float32) ** level_of(key_of[6], (SECTIONS, D, KVW), ((0, 32), (2, 4)), -0.2, 0.2)), 0.01, 1.0)
    output_second = jnp.clip(jnp.exp(math.log(1.0) - 4.6051702 * jax.random.uniform(key_of[7], (SECTIONS, D, KVW), jnp.float32) ** level_of(key_of[7], (SECTIONS, D, KVW), ((0, 32), (2, 4)), -0.2, 0.2)), 0.01, 1.0)
    layer_map = draw_layer_map(jax.random.fold_in(key_of[11], 71), 0)
    old_section = draw_old_section(jax.random.fold_in(key_of[11], 71), 0)
    new_section = draw_new_section(jax.random.fold_in(key_of[11], 71), 0)
    return dict(tokens=tokens, cotangent=cotangent, value_weight=value_weight, output_weight=output_weight, value_first=value_first, output_first=output_first, value_second=value_second, output_second=output_second, layer_map=layer_map, old_section=old_section, new_section=new_section)


epsilon = 1e-05
beta_one = 0.9
beta_two = 0.95
step_rate = 0.003
adam_floor = 1e-08

def normalize(stream):
    widened = stream.astype(jnp.float32)
    factor = lax.rsqrt(lax.optimization_barrier(jnp.mean(widened * widened, axis=-1, keepdims=True)) + epsilon)
    return (widened * factor, factor)

def forward_layer(stream, value_full, output_full):
    normed, factor = normalize(stream)
    hidden = normed.astype(jnp.bfloat16)
    preact = jnp.dot(hidden, value_full, preferred_element_type=jnp.float32)
    unit_values = jax.nn.silu(preact).astype(jnp.bfloat16)
    mixing = lax.dot_general(unit_values, output_full, (((1,), (1,)), ((), ())), preferred_element_type=jnp.float32)
    return ((stream.astype(jnp.float32) + mixing).astype(jnp.bfloat16), preact, unit_values)

def backward_layer(stream, preact, grad_out, value_full, output_full):
    grad_units = jnp.dot(grad_out, output_full, preferred_element_type=jnp.float32)
    gate_value = jax.nn.sigmoid(preact)
    grad_inner = (grad_units * gate_value * (1.0 + preact * (1.0 - gate_value))).astype(jnp.bfloat16)
    grad_hidden = lax.dot_general(grad_inner, value_full, (((1,), (1,)), ((), ())), preferred_element_type=jnp.float32)
    normed, factor = normalize(stream)
    grad_stream = factor * (grad_hidden - normed * lax.optimization_barrier(jnp.mean(grad_hidden * normed, axis=-1, keepdims=True)))
    return ((grad_out.astype(jnp.float32) + grad_stream).astype(jnp.bfloat16), grad_inner)

def adam_update(weight, first, second, gradient):
    first_new = beta_one * first + (1.0 - beta_one) * gradient
    second_new = beta_two * second + (1.0 - beta_two) * gradient * gradient
    weight_new = (weight.astype(jnp.float32) - step_rate * first_new / (jnp.sqrt(second_new) + adam_floor)).astype(jnp.bfloat16)
    return (weight_new, first_new, second_new)

def reference(tokens, cotangent, value_weight, output_weight, value_first, output_first, value_second, output_second, layer_map, old_section, new_section):
    layer_count = layer_map.shape[0]
    sources = []
    saved_layers = []
    stream = tokens
    for layer_index in range(layer_count):
        source = old_section[layer_map[layer_index]]
        sources.append(source)
        result, preact, unit_values = forward_layer(stream, value_weight[source], output_weight[source])
        saved_layers.append((stream, preact, unit_values))
        stream = result
    flowing = cotangent
    outputs = [jnp.zeros(value_weight.shape, jnp.bfloat16), jnp.zeros(value_weight.shape, jnp.bfloat16), jnp.zeros(value_weight.shape, jnp.float32), jnp.zeros(value_weight.shape, jnp.float32), jnp.zeros(value_weight.shape, jnp.float32), jnp.zeros(value_weight.shape, jnp.float32)]
    for layer_index in reversed(range(layer_count)):
        source = sources[layer_index]
        stream_in, preact, unit_values = saved_layers[layer_index]
        result, grad_inner = backward_layer(stream_in, preact, flowing, value_weight[source], output_weight[source])
        hidden = normalize(stream_in)[0].astype(jnp.bfloat16)
        grad_value = lax.dot_general(hidden, grad_inner, (((0,), (0,)), ((), ())), preferred_element_type=jnp.float32)
        grad_output = lax.dot_general(flowing, unit_values, (((0,), (0,)), ((), ())), preferred_element_type=jnp.float32)
        value_new = adam_update(value_weight[source], value_first[source], value_second[source], grad_value)
        output_new = adam_update(output_weight[source], output_first[source], output_second[source], grad_output)
        target = new_section[layer_index]
        outputs[0] = outputs[0].at[target].set(value_new[0])
        outputs[1] = outputs[1].at[target].set(output_new[0])
        outputs[2] = outputs[2].at[target].set(value_new[1])
        outputs[3] = outputs[3].at[target].set(output_new[1])
        outputs[4] = outputs[4].at[target].set(value_new[2])
        outputs[5] = outputs[5].at[target].set(output_new[2])
        flowing = result
    return (outputs[0], outputs[1], outputs[2], outputs[3], outputs[4], outputs[5])
```

```python
import jax
import jax.numpy as jnp
from jax import lax
from jax.experimental import pallas as pl
from jax.experimental.pallas import tpu as pltpu
from jax.sharding import PartitionSpec as P

epsilon = 1e-05
beta_one = 0.9
beta_two = 0.95
step_rate = 0.003
adam_floor = 1e-08
f32 = jnp.float32
bf16 = jnp.bfloat16
both = ("section", "tp")
rows = 8


def value_of(w):
    return jnp.concatenate([w[:, z, 0, 0].reshape(-1, w.shape[-1]) for z in range(w.shape[1])], axis=1)


def output_of(w):
    return jnp.concatenate([w[:, z, 0, 1].reshape(-1, w.shape[-1]) for z in range(w.shape[1])], axis=1)


def forward_kernel(map_ref, x_ref, w_ref, in_ref, hid_ref, pre_ref, unit_ref, state):
    @pl.when(pl.program_id(0) == 0)
    def _():
        state[...] = x_ref[...]

    x = state[...]
    in_ref[0] = x.astype(bf16)
    factor = lax.rsqrt(jnp.mean(x * x, axis=-1, keepdims=True) + epsilon)
    hidden = (x * factor).astype(bf16)
    hid_ref[0] = hidden
    w = w_ref[...]
    pre = jnp.dot(hidden, value_of(w), preferred_element_type=f32)
    pre_ref[0] = pre
    units = jax.nn.silu(pre).astype(bf16)
    unit_ref[0] = units
    mixing = lax.dot_general(units, output_of(w), (((1,), (1,)), ((), ())), preferred_element_type=f32)
    state[...] = (x + mixing).astype(bf16).astype(f32)


def backward_kernel(map_ref, g_ref, w_ref, in_ref, pre_ref, out_g_ref, out_z_ref, state):
    @pl.when(pl.program_id(0) == 0)
    def _():
        state[...] = g_ref[...]

    g = state[...]
    gb = g.astype(bf16)
    out_g_ref[0] = gb
    w = w_ref[...]
    gu = jnp.dot(gb, output_of(w), preferred_element_type=f32)
    pre = pre_ref[0]
    s = jax.nn.sigmoid(pre)
    gz = (gu * s * (1.0 + pre * (1.0 - s))).astype(bf16)
    out_z_ref[0] = gz
    gh = lax.dot_general(gz, value_of(w), (((1,), (1,)), ((), ())), preferred_element_type=f32)
    x = in_ref[0].astype(f32)
    factor = lax.rsqrt(jnp.mean(x * x, axis=-1, keepdims=True) + epsilon)
    n = x * factor
    gs = factor * (gh - n * jnp.mean(gh * n, axis=-1, keepdims=True))
    state[...] = (g + gs).astype(bf16).astype(f32)


def run_layers(kernel, layer_map, start, weights, extra, outs, backward):
    new = layer_map.shape[0]
    at = (lambda j: new - 1 - j) if backward else (lambda j: j)
    wshape = weights.shape

    def per_layer(a):
        return pl.BlockSpec((1,) + a.shape[1:], lambda j, m: (at(j), 0, 0))

    size = 2 * wshape[0] * wshape[1] * 2 * wshape[4] * wshape[5]
    return pl.pallas_call(
        kernel,
        grid_spec=pltpu.PrefetchScalarGridSpec(
            num_scalar_prefetch=1,
            grid=(new,),
            in_specs=[
                pl.BlockSpec(start.shape, lambda j, m: (0, 0)),
                pl.BlockSpec(
                    (wshape[0], wshape[1], 1) + wshape[3:], lambda j, m: (0, 0, m[at(j)], 0, 0, 0)
                ),
            ]
            + [per_layer(a) for a in extra],
            out_specs=[per_layer(a) for a in outs],
            scratch_shapes=[pltpu.VMEM(start.shape, f32)],
        ),
        out_shape=outs,
        compiler_params=pltpu.CompilerParams(
            dimension_semantics=("arbitrary",), vmem_limit_bytes=48 * 2**20
        ),
        cost_estimate=pl.CostEstimate(
            flops=new * 4 * rows * size // 4, bytes_accessed=new * size, transcendentals=0
        ),
    )(layer_map, start, weights, *extra)


def pick_kernel(index_ref, keep_ref, in_ref, out_ref):
    def one(k, carry):
        kept = in_ref[index_ref[k]] * keep_ref[k].astype(f32).astype(bf16)
        out_ref[k] = kept
        return carry

    lax.fori_loop(0, out_ref.shape[0], one, 0)


def pick_slots(index, keep, pieces):
    whole = pl.BlockSpec(memory_space=pltpu.VMEM)
    scalar = pl.BlockSpec(memory_space=pltpu.SMEM)
    flat = pieces.reshape(pieces.shape[0], -1, pieces.shape[-1])
    got = pl.pallas_call(
        pick_kernel,
        in_specs=[scalar, scalar, whole],
        out_specs=whole,
        out_shape=jax.ShapeDtypeStruct((index.shape[0],) + flat.shape[1:], bf16),
        compiler_params=pltpu.CompilerParams(vmem_limit_bytes=24 * 2**20),
    )(index, keep, flat)
    return got.reshape((index.shape[0],) + pieces.shape[1:])


def pick(onehot, pieces):
    flat = pieces.reshape(pieces.shape[0], -1, pieces.shape[-1])
    got = lax.dot_general(onehot, flat, (((1,), (0,)), ((), ())), preferred_element_type=bf16)
    return got.reshape((onehot.shape[0],) + pieces.shape[1:])


def adam_update(weight, first, second, gradient, owned):
    first_new = beta_one * first + (1.0 - beta_one) * gradient
    second_new = beta_two * second + (1.0 - beta_two) * gradient * gradient
    weight_new = weight - step_rate * first_new / (jnp.sqrt(second_new) + adam_floor)
    weight_new = jnp.where(owned, weight_new, 0.0).astype(bf16)
    return (weight_new[None], first_new[None], second_new[None])


def body(
    tokens,
    cotangent,
    value_weight,
    output_weight,
    value_first,
    output_first,
    value_second,
    output_second,
    layer_map,
    old_section,
    new_section,
):
    sections = lax.axis_size("section")
    width = lax.axis_size("tp")
    myself = lax.axis_index("section")
    column = lax.axis_index("tp")
    new = new_section.shape[0]
    features, channels = value_weight.shape[1:]
    part = features // sections
    positions = lax.iota(jnp.int32, sections)
    owner_match = positions[:, None] == new_section[None, :]
    map_match = layer_map[:, None] == lax.iota(jnp.int32, old_section.shape[0])[None, :]
    source = jnp.sum(jnp.where(map_match, old_section[None, :], 0), axis=1)
    holds = jnp.any(owner_match, axis=1)
    wanted = jnp.sum(jnp.where(owner_match, source[None, :], 0), axis=1)
    send_layer = owner_match.astype(bf16)
    owned = jnp.any(new_section == myself)
    my_layer = jnp.sum(jnp.where(new_section == myself, lax.iota(jnp.int32, new), 0))
    my_old = jnp.sum(jnp.where(lax.iota(jnp.int32, new) == my_layer, layer_map, 0))

    def pieces_of(arrays):
        return jnp.stack([a.reshape(sections, part, channels).astype(bf16) for a in arrays], axis=1)

    def spread(a):
        return lax.all_to_all(a, "section", split_axis=0, concat_axis=0, tiled=True)

    weight_pieces = pick_slots(
        old_section, jnp.ones_like(old_section), spread(pieces_of((value_weight, output_weight)))
    )
    gathered = lax.all_gather(weight_pieces, both)
    gathered = gathered.reshape((sections, width) + weight_pieces.shape)

    moments = pick_slots(
        wanted,
        holds.astype(jnp.int32),
        spread(pieces_of((value_first, output_first, value_second, output_second))),
    )
    moments = spread(moments)

    count = tokens.shape[0] // sections

    def mine(a):
        block = lax.dynamic_slice_in_dim(a, myself * count, count, axis=0).astype(f32)
        return jnp.pad(block, ((0, rows - count), (0, 0)))

    inner = width * channels
    shape = jax.ShapeDtypeStruct
    saved_in, hidden, pre, units = run_layers(
        forward_kernel,
        layer_map,
        mine(tokens),
        gathered,
        (),
        [
            shape((new, rows, features), bf16),
            shape((new, rows, features), bf16),
            shape((new, rows, inner), f32),
            shape((new, rows, inner), bf16),
        ],
        False,
    )
    grads, inner_grads = run_layers(
        backward_kernel,
        layer_map,
        mine(cotangent),
        gathered,
        (saved_in, pre),
        [shape((new, rows, features), bf16), shape((new, rows, inner), bf16)],
        True,
    )

    def to_owner(wide, narrow):
        w = pick(send_layer, wide[:, :count])
        n = pick(send_layer, narrow[:, :count])
        n = n.reshape(sections, count, width, channels).transpose(0, 2, 1, 3)
        w = jnp.broadcast_to(w[:, None], (sections, width, count, features))
        message = jnp.concatenate([w, n], axis=-1).reshape(sections * width, count, features + channels)
        got = lax.all_to_all(message, both, split_axis=0, concat_axis=0, tiled=True)
        got = got.reshape(sections * width * count, features + channels)
        return got[:, :features], got[:, features:]

    hidden_all, units_all = to_owner(hidden, units)
    grads_all, inner_all = to_owner(grads, inner_grads)

    def weight_grad(a, b):
        return lax.dot_general(a, b, (((0,), (0,)), ((), ())), preferred_element_type=f32)

    grad_value = weight_grad(hidden_all, inner_all)
    grad_output = weight_grad(grads_all, units_all)
    own = lax.dynamic_slice(
        gathered, (0, column, my_old, 0, 0, 0), (sections, 1, 1, 2, part, channels)
    )
    own = own.reshape(sections, 2, part, channels).astype(f32)
    moments = moments.astype(f32)

    def full(a):
        return a.reshape(features, channels)

    value_new = adam_update(full(own[:, 0]), full(moments[:, 0]), full(moments[:, 2]), grad_value, owned)
    output_new = adam_update(full(own[:, 1]), full(moments[:, 1]), full(moments[:, 3]), grad_output, owned)
    return (value_new[0], output_new[0], value_new[1], output_new[1], value_new[2], output_new[2])


def solution(mesh):
    split = P("section", None, "tp")
    placed = (P("tp", None),) * 2 + (split,) * 6 + (P(),) * 3
    return jax.shard_map(body, mesh=mesh, in_specs=placed, out_specs=(split,) * 6, check_vma=False)
```

```python
import jax
import jax.numpy as jnp
from jax import lax
from jax.experimental import pallas as pl
from jax.experimental.pallas import tpu as pltpu
from jax.sharding import Mesh
from jax.sharding import PartitionSpec as P

epsilon = 1e-05
beta_one = 0.9
beta_two = 0.95
step_rate = 0.003
adam_floor = 1e-08
f32 = jnp.float32
bf16 = jnp.bfloat16
section = ("y", "x", "c")
both = ("y", "x", "c", "z")
orders = (("x", "y", "z"), ("y", "z", "x"), ("z", "x", "y"))
ring = 4
groups = 3
chunk = 3
rows = 8
MESH = pl.DeviceIdType.MESH


def unit_counts(units):
    return [(units - g + groups - 1) // groups for g in range(groups)]


def gather_kernel(counts, own_ref, out_ref, send, recv, own_sem):
    me = {a: lax.axis_index(a) for a in both}

    def beside(axis, step):
        size = 2 if axis == "c" else ring
        return {axis: lax.rem(me[axis] + step + size, size)}

    barrier = pltpu.get_barrier_semaphore()
    partners = [beside(a, s) for a in ("x", "y", "z") for s in (1, -1)] + [beside("c", 1)]
    for p in partners:
        pl.semaphore_signal(barrier, inc=1, device_id=p, device_id_type=MESH)
    pl.semaphore_wait(barrier, len(partners))

    used = [0]
    started = []

    def push(src, dst, to):
        n = used[0]
        used[0] += 1
        copy = pltpu.make_async_remote_copy(
            src_ref=src,
            dst_ref=dst,
            send_sem=send.at[n],
            recv_sem=recv.at[n],
            device_id=to,
            device_id_type=MESH,
        )
        copy.start()
        started.append(copy)
        return copy

    def place(g, phase, lo, size, at, half):
        full = list(orders[g][:phase])
        axis = orders[g][phase]
        index = {a: pl.ds(me[a], 1) for a in ("x", "y", "z")}
        for a in full:
            index[a] = pl.ds(0, ring)
        index[axis] = pl.ds(at, 1)
        if half is not None:
            if full:
                index[full[0]] = pl.ds(half * (ring // 2), ring // 2)
            else:
                cut = size // 2
                lo, size = (lo, cut) if half == 0 else (lo + cut, size - cut)
        return out_ref.at[g, pl.ds(lo, size), me["c"], index["x"], index["y"], index["z"]]

    def first(g, phase, lo, size):
        axis = orders[g][phase]
        here = place(g, phase, lo, size, me[axis], None)
        return [push(here, here, beside(axis, s)) for s in (1, -1)]

    def second(g, phase, lo, size, copies):
        axis = orders[g][phase]
        for c in copies:
            c.wait_recv()
        out = []
        for half, s in ((0, 1), (1, -1)):
            at = lax.rem(me[axis] - s + ring, ring)
            part = place(g, phase, lo, size, at, half)
            out.append(push(part, part, beside(axis, s)))
        return out

    mine = pltpu.make_async_copy(
        own_ref, out_ref.at[:, :, me["c"], me["x"], me["y"], me["z"]], own_sem
    )
    mine.start()
    mine.wait()
    for phase in range(2):
        copies = [first(g, phase, 0, counts[g]) for g in range(groups)]
        copies = [second(g, phase, 0, counts[g], copies[g]) for g in range(groups)]
        for pair in copies:
            for c in pair:
                c.wait_recv()
    spans = [[(lo, min(chunk, n - lo)) for lo in range(0, n, chunk)] for n in counts]
    total = max(len(x) for x in spans)
    sent, halves, crossing = {}, {}, []

    def begin(j):
        for g in range(groups):
            if j < len(spans[g]):
                sent[g, j] = first(g, 2, *spans[g][j])

    def cross(j):
        for g in range(groups):
            if (g, j) in halves:
                for c in halves[g, j]:
                    c.wait_recv()
                lo, size = spans[g][j]
                block = out_ref.at[g, pl.ds(lo, size), me["c"]]
                crossing.append(push(block, block, beside("c", 1)))

    begin(0)
    begin(1)
    for j in range(total):
        for g in range(groups):
            if (g, j) in sent:
                halves[g, j] = second(g, 2, *spans[g][j], sent[g, j])
        begin(j + 2)
        if j:
            cross(j - 1)
    cross(total - 1)
    for c in crossing:
        c.wait_recv()
    for c in started:
        c.wait_send()


def gather(own, units):
    counts = unit_counts(units)
    copies = sum(8 + 5 * -(-n // chunk) for n in counts)
    part, channels = own.shape[-2:]
    return pl.pallas_call(
        lambda *refs: gather_kernel(counts, *refs),
        in_specs=[pl.BlockSpec(memory_space=pl.ANY)],
        out_specs=pl.BlockSpec(memory_space=pl.ANY),
        out_shape=jax.ShapeDtypeStruct(own.shape[:2] + (2, ring, ring, ring, part, channels), bf16),
        scratch_shapes=[
            pltpu.SemaphoreType.DMA((copies,)),
            pltpu.SemaphoreType.DMA((copies,)),
            pltpu.SemaphoreType.DMA,
        ],
        compiler_params=pltpu.CompilerParams(
            collective_id=0, has_side_effects=True, vmem_limit_bytes=16 * 2**20
        ),
        cost_estimate=pl.CostEstimate(flops=0, bytes_accessed=400 * 2**20, transcendentals=0),
    )(own)


def wide(w):
    w = w[0, 0]
    return jnp.concatenate([w[:, z].reshape(-1, w.shape[-1]) for z in range(w.shape[1])], axis=1)


def forward_kernel(map_ref, x_ref, v_ref, o_ref, in_ref, hid_ref, pre_ref, unit_ref, state):
    @pl.when(pl.program_id(0) == 0)
    def _():
        state[...] = x_ref[...]

    x = state[...]
    in_ref[0] = x.astype(bf16)
    factor = lax.rsqrt(jnp.mean(x * x, axis=-1, keepdims=True) + epsilon)
    hidden = (x * factor).astype(bf16)
    hid_ref[0] = hidden
    pre = jnp.dot(hidden, wide(v_ref[...]), preferred_element_type=f32)
    pre_ref[0] = pre
    units = jax.nn.silu(pre).astype(bf16)
    unit_ref[0] = units
    mixing = lax.dot_general(units, wide(o_ref[...]), (((1,), (1,)), ((), ())), preferred_element_type=f32)
    state[...] = (x + mixing).astype(bf16).astype(f32)


def backward_kernel(map_ref, g_ref, v_ref, o_ref, in_ref, pre_ref, out_g_ref, out_z_ref, state):
    @pl.when(pl.program_id(0) == 0)
    def _():
        state[...] = g_ref[...]

    g = state[...]
    gb = g.astype(bf16)
    out_g_ref[0] = gb
    gu = jnp.dot(gb, wide(o_ref[...]), preferred_element_type=f32)
    pre = pre_ref[0]
    s = jax.nn.sigmoid(pre)
    gz = (gu * s * (1.0 + pre * (1.0 - s))).astype(bf16)
    out_z_ref[0] = gz
    gh = lax.dot_general(gz, wide(v_ref[...]), (((1,), (1,)), ((), ())), preferred_element_type=f32)
    x = in_ref[0].astype(f32)
    factor = lax.rsqrt(jnp.mean(x * x, axis=-1, keepdims=True) + epsilon)
    n = x * factor
    gs = factor * (gh - n * jnp.mean(gh * n, axis=-1, keepdims=True))
    state[...] = (g + gs).astype(bf16).astype(f32)


def run_layers(kernel, layer_map, start, weights, extra, outs, backward):
    new = layer_map.shape[0]
    at = (lambda j: new - 1 - j) if backward else (lambda j: j)
    wshape = weights.shape

    def per_layer(a):
        return pl.BlockSpec((1,) + a.shape[1:], lambda j, m: (at(j), 0, 0))

    def half(which):
        def index(j, m):
            unit = 2 * m[at(j)] + which
            return (lax.rem(unit, groups), lax.div(unit, groups), 0, 0, 0, 0)

        return pl.BlockSpec((1, 1) + wshape[2:], index)

    size = 4 * wshape[2] * wshape[3] * wshape[4] * wshape[5]
    return pl.pallas_call(
        kernel,
        grid_spec=pltpu.PrefetchScalarGridSpec(
            num_scalar_prefetch=1,
            grid=(new,),
            in_specs=[
                pl.BlockSpec(start.shape, lambda j, m: (0, 0)),
                half(0),
                half(1),
            ]
            + [per_layer(a) for a in extra],
            out_specs=[per_layer(a) for a in outs],
            scratch_shapes=[pltpu.VMEM(start.shape, f32)],
        ),
        out_shape=outs,
        compiler_params=pltpu.CompilerParams(
            dimension_semantics=("arbitrary",), vmem_limit_bytes=48 * 2**20
        ),
        cost_estimate=pl.CostEstimate(
            flops=new * 4 * rows * size // 4, bytes_accessed=new * size, transcendentals=0
        ),
    )(layer_map, start, weights, weights, *extra)


def pick_kernel(index_ref, keep_ref, in_ref, out_ref):
    def one(k, carry):
        kept = in_ref[index_ref[k]] * keep_ref[k].astype(f32).astype(bf16)
        out_ref[k] = kept
        return carry

    lax.fori_loop(0, out_ref.shape[0], one, 0)


def pick_slots(index, keep, pieces):
    whole = pl.BlockSpec(memory_space=pltpu.VMEM)
    scalar = pl.BlockSpec(memory_space=pltpu.SMEM)
    flat = pieces.reshape(pieces.shape[0], -1, pieces.shape[-1])
    got = pl.pallas_call(
        pick_kernel,
        in_specs=[scalar, scalar, whole],
        out_specs=whole,
        out_shape=jax.ShapeDtypeStruct((index.shape[0],) + flat.shape[1:], bf16),
        compiler_params=pltpu.CompilerParams(vmem_limit_bytes=24 * 2**20),
    )(index, keep, flat)
    return got.reshape((index.shape[0],) + pieces.shape[1:])


def pick(onehot, pieces):
    flat = pieces.reshape(pieces.shape[0], -1, pieces.shape[-1])
    got = lax.dot_general(onehot, flat, (((1,), (0,)), ((), ())), preferred_element_type=bf16)
    return got.reshape((onehot.shape[0],) + pieces.shape[1:])


def adam_update(weight, first, second, gradient, owned):
    first_new = beta_one * first + (1.0 - beta_one) * gradient
    second_new = beta_two * second + (1.0 - beta_two) * gradient * gradient
    weight_new = weight - step_rate * first_new / (jnp.sqrt(second_new) + adam_floor)
    weight_new = jnp.where(owned, weight_new, 0.0).astype(bf16)
    return (weight_new[None], first_new[None], second_new[None])


def body(
    tokens,
    cotangent,
    value_weight,
    output_weight,
    value_first,
    output_first,
    value_second,
    output_second,
    layer_map,
    old_section,
    new_section,
):
    sections = lax.axis_size(section)
    width = lax.axis_size("z")
    myself = lax.axis_index(section)
    column = lax.axis_index("z")
    new = new_section.shape[0]
    features, channels = value_weight.shape[1:]
    part = features // sections
    positions = lax.iota(jnp.int32, sections)
    owner_match = positions[:, None] == new_section[None, :]
    map_match = layer_map[:, None] == lax.iota(jnp.int32, old_section.shape[0])[None, :]
    source = jnp.sum(jnp.where(map_match, old_section[None, :], 0), axis=1)
    holds = jnp.any(owner_match, axis=1)
    wanted = jnp.sum(jnp.where(owner_match, source[None, :], 0), axis=1)
    send_layer = owner_match.astype(bf16)
    owned = jnp.any(new_section == myself)
    my_layer = jnp.sum(jnp.where(new_section == myself, lax.iota(jnp.int32, new), 0))
    my_old = jnp.sum(jnp.where(lax.iota(jnp.int32, new) == my_layer, layer_map, 0))

    def pieces_of(arrays):
        return jnp.stack([a.reshape(sections, part, channels).astype(bf16) for a in arrays], axis=1)

    def spread(a):
        return lax.all_to_all(a, section, split_axis=0, concat_axis=0, tiled=True)

    def turned(a):
        return a.reshape(2, ring, ring, part * channels).transpose(2, 1, 0, 3)

    old = old_section.shape[0]
    pieces = spread(pieces_of((turned(value_weight), turned(output_weight))))
    deep = unit_counts(2 * old)[0]
    unit = jnp.minimum(
        groups * lax.iota(jnp.int32, deep)[None, :] + lax.iota(jnp.int32, groups)[:, None], 2 * old - 1
    ).reshape(-1)
    unit_match = (unit // 2)[:, None] == lax.iota(jnp.int32, old)[None, :]
    slots = 2 * jnp.sum(jnp.where(unit_match, old_section[None, :], 0), axis=1) + unit % 2
    own = pick_slots(slots, jnp.ones_like(slots), pieces.reshape(2 * sections, part, channels))
    gathered = gather(own.reshape(groups, deep, part, channels), 2 * old)
    gathered = gathered.reshape(groups, deep, sections, width, part, channels)

    moments = pick_slots(
        wanted,
        holds.astype(jnp.int32),
        spread(pieces_of((value_first, output_first, value_second, output_second))),
    )
    moments = spread(moments)

    count = tokens.shape[0] // sections

    def mine(a):
        block = lax.dynamic_slice_in_dim(a, myself * count, count, axis=0).astype(f32)
        return jnp.pad(block, ((0, rows - count), (0, 0)))

    inner = width * channels
    shape = jax.ShapeDtypeStruct
    saved_in, hidden, pre, units = run_layers(
        forward_kernel,
        layer_map,
        mine(tokens),
        gathered,
        (),
        [
            shape((new, rows, features), bf16),
            shape((new, rows, features), bf16),
            shape((new, rows, inner), f32),
            shape((new, rows, inner), bf16),
        ],
        False,
    )
    grads, inner_grads = run_layers(
        backward_kernel,
        layer_map,
        mine(cotangent),
        gathered,
        (saved_in, pre),
        [shape((new, rows, features), bf16), shape((new, rows, inner), bf16)],
        True,
    )

    def to_owner(wide, narrow):
        w = pick(send_layer, wide[:, :count])
        n = pick(send_layer, narrow[:, :count])
        n = n.reshape(sections, count, width, channels).transpose(0, 2, 1, 3)
        w = jnp.broadcast_to(w[:, None], (sections, width, count, features))
        message = jnp.concatenate([w, n], axis=-1).reshape(sections * width, count, features + channels)
        got = lax.all_to_all(message, both, split_axis=0, concat_axis=0, tiled=True)
        got = got.reshape(sections * width * count, features + channels)
        return got[:, :features], got[:, features:]

    hidden_all, units_all = to_owner(hidden, units)
    grads_all, inner_all = to_owner(grads, inner_grads)

    def weight_grad(a, b):
        return lax.dot_general(a, b, (((0,), (0,)), ((), ())), preferred_element_type=f32)

    grad_value = weight_grad(hidden_all, inner_all)
    grad_output = weight_grad(grads_all, units_all)
    def own_of(which):
        unit = 2 * my_old + which
        got = lax.dynamic_slice(
            gathered,
            (unit % groups, unit // groups, 0, column, 0, 0),
            (1, 1, sections, 1, part, channels),
        )
        return got.reshape(features, channels).astype(f32)

    moments = moments.astype(f32)

    def full(a):
        return a.reshape(features, channels)

    value_new = adam_update(own_of(0), full(moments[:, 0]), full(moments[:, 2]), grad_value, owned)
    output_new = adam_update(own_of(1), full(moments[:, 1]), full(moments[:, 3]), grad_output, owned)
    return (value_new[0], output_new[0], value_new[1], output_new[1], value_new[2], output_new[2])


def solution(mesh):
    split = P(section, None, "z")
    placed = (P("z", None),) * 2 + (split,) * 6 + (P(),) * 3
    fine = Mesh(mesh.devices.reshape(ring, ring, 2, ring), both)
    return jax.shard_map(body, mesh=fine, in_specs=placed, out_specs=(split,) * 6, check_vma=False)
```

```python
import jax
import jax.numpy as jnp
from jax import lax
from jax.experimental import pallas as pl
from jax.experimental.pallas import tpu as pltpu
from jax.sharding import Mesh
from jax.sharding import PartitionSpec as P

epsilon = 1e-05
beta_one = 0.9
beta_two = 0.95
step_rate = 0.003
adam_floor = 1e-08
f32 = jnp.float32
bf16 = jnp.bfloat16
section = ("y", "x", "c")
both = ("y", "x", "c", "z")
orders = (("x", "y", "z"), ("y", "z", "x"), ("z", "x", "y"))
ring = 4
groups = 3
rows = 8
MESH = pl.DeviceIdType.MESH


def deep_of(units):
    return -(-units // groups)


def forward_layer(x, value, output):
    factor = lax.rsqrt(jnp.mean(x * x, axis=-1, keepdims=True) + epsilon)
    hidden = (x * factor).astype(bf16)
    pre = jnp.dot(hidden, value, preferred_element_type=f32)
    units = jax.nn.silu(pre).astype(bf16)
    mixing = lax.dot_general(units, output, (((1,), (1,)), ((), ())), preferred_element_type=f32)
    return (x + mixing).astype(bf16).astype(f32), hidden, pre, units


def gather_kernel(
    old,
    twice_ref,
    own_ref,
    x_ref,
    out_ref,
    in_ref,
    hid_ref,
    pre_ref,
    unit_ref,
    held,
    state,
    send_one,
    recv_one,
    send,
    recv,
    load_sem,
    own_sem,
):
    deep = deep_of(2 * old)
    me = {a: lax.axis_index(a) for a in both}

    def beside(axis, step):
        size = 2 if axis == "c" else ring
        return {axis: lax.rem(me[axis] + step + size, size)}

    barrier = pltpu.get_barrier_semaphore()
    partners = [beside(a, s) for a in ("x", "y", "z") for s in (1, -1)] + [beside("c", 1)]
    for p in partners:
        pl.semaphore_signal(barrier, inc=1, device_id=p, device_id_type=MESH)
    pl.semaphore_wait(barrier, len(partners))

    def copy(src, dst, to, send_sem, recv_sem):
        return pltpu.make_async_remote_copy(
            src_ref=src,
            dst_ref=dst,
            send_sem=send_sem,
            recv_sem=recv_sem,
            device_id=to,
            device_id_type=MESH,
        )

    def place(g, phase, k, at, half):
        full = orders[g][:phase]
        axis = orders[g][phase]
        index = dict(me)
        for a in full:
            index[a] = pl.ds(0, ring)
        if half is not None and full:
            index[full[0]] = pl.ds(half * (ring // 2), ring // 2)
        index[axis] = at
        return out_ref.at[g, k, me["c"], index["x"], index["y"], index["z"]]

    def bulk_first(g):
        axis = orders[g][0]
        dst = place(g, 0, pl.ds(0, deep), me[axis], None)
        return [
            copy(own_ref.at[g], dst, beside(axis, s), send_one.at[g, n], recv_one.at[g, n])
            for n, s in ((0, 1), (1, -1))
        ]

    def bulk_second(g):
        axis = orders[g][0]
        cut = deep // 2
        out = []
        for n, s, lo, size in ((2, 1, 0, cut), (3, -1, cut, deep - cut)):
            part = place(g, 0, pl.ds(lo, size), lax.rem(me[axis] - s + ring, ring), None)
            out.append(copy(part, part, beside(axis, s), send_one.at[g, n], recv_one.at[g, n]))
        return out

    def first(g, phase, k):
        axis = orders[g][phase]
        here = place(g, phase, k, me[axis], None)
        base = 4 * (phase - 1)
        return [
            copy(here, here, beside(axis, s), send.at[g, k, base + n], recv.at[g, k, base + n])
            for n, s in ((0, 1), (1, -1))
        ]

    def second(g, phase, k):
        axis = orders[g][phase]
        base = 4 * (phase - 1) + 2
        out = []
        for n, s in ((0, 1), (1, -1)):
            part = place(g, phase, k, lax.rem(me[axis] - s + ring, ring), n)
            out.append(copy(part, part, beside(axis, s), send.at[g, k, base + n], recv.at[g, k, base + n]))
        return out

    def cross(g, k):
        block = out_ref.at[g, k, me["c"]]
        return [copy(block, block, beside("c", 1), send.at[g, k, 8], recv.at[g, k, 8])]

    def start(copies):
        for c in copies:
            c.start()

    def arrived(copies):
        for c in copies:
            c.wait_recv()

    def each(k, before, after, *more):
        for g in range(groups):
            if before is not None:
                arrived(before(g, *more, k))
            start(after(g, *more, k))

    def spread_start(k):
        each(k, None, lambda g, k: first(g, 1, k))

    def spread_pass(k):
        each(k, lambda g, k: first(g, 1, k), lambda g, k: second(g, 1, k))

    def plane_start(k):
        each(k, lambda g, k: second(g, 1, k), lambda g, k: first(g, 2, k))

    def plane_pass(k):
        each(k, lambda g, k: first(g, 2, k), lambda g, k: second(g, 2, k))

    def cross_start(k):
        each(k, lambda g, k: second(g, 2, k), cross)

    def load(g, k):
        unit = groups * k + g
        layer = lax.div(unit, 2)
        return pltpu.make_async_copy(
            out_ref.at[g, k], held.at[lax.rem(layer, 2), lax.rem(unit, 2)], load_sem.at[g]
        )

    def evaluate(q, carry):
        layer = lax.div(q, 2)
        again = lax.rem(q, 2)
        slot = lax.rem(layer, 2)
        x = state[...]
        following, hidden, pre, units = forward_layer(x, wide(held[slot, 0]), wide(held[slot, 1]))
        in_ref[q] = x.astype(bf16)
        hid_ref[q] = hidden
        pre_ref[q] = pre
        unit_ref[q] = units
        keep = jnp.maximum(twice_ref[layer], 1 - again) > 0
        state[...] = jnp.where(keep, following, x)
        return carry

    def use(k):
        for g in range(groups):
            arrived(cross(g, k))
            load(g, k).start()
        for g in range(groups):
            load(g, k).wait()
        done = jnp.minimum(lax.div(groups * k + groups, 2), old)
        lax.fori_loop(2 * lax.div(groups * k, 2), 2 * done, evaluate, 0)

    mine = pltpu.make_async_copy(
        own_ref, out_ref.at[:, :, me["c"], me["x"], me["y"], me["z"]], own_sem
    )
    mine.start()
    for g in range(groups):
        start(bulk_first(g))
    state[...] = x_ref[...]
    for g in range(groups):
        arrived(bulk_first(g))
        start(bulk_second(g))
    mine.wait()
    for g in range(groups):
        arrived(bulk_second(g))
    for k in range(4):
        spread_start(k)
    for k in range(3):
        spread_pass(k)
    for k in range(2):
        plane_start(k)

    def step(t, carry):
        def at(k, act):
            @pl.when((k >= 0) & (k < deep))
            def _():
                act(k)

        at(t, plane_pass)
        at(t + 2, plane_start)
        at(t + 3, spread_pass)
        at(t + 4, spread_start)
        at(t - 1, cross_start)
        at(t - 2, use)
        return carry

    lax.fori_loop(0, deep + 2, step, 0)

    for g in range(groups):
        for c in bulk_first(g) + bulk_second(g):
            c.wait_send()

    def drain(k, carry):
        for g in range(groups):
            for phase in (1, 2):
                for c in first(g, phase, k) + second(g, phase, k):
                    c.wait_send()
            for c in cross(g, k):
                c.wait_send()
        return carry

    lax.fori_loop(0, deep, drain, 0)


def gather_forward(twice, own, x):
    old = twice.shape[0]
    deep, part, channels = own.shape[-3:]
    features = x.shape[1]
    inner = ring * channels
    shape = jax.ShapeDtypeStruct
    vmem = pl.BlockSpec(memory_space=pltpu.VMEM)
    hbm = pl.BlockSpec(memory_space=pl.ANY)
    unit = (2, ring, ring, ring, part, channels)
    return pl.pallas_call(
        lambda *refs: gather_kernel(old, *refs),
        in_specs=[pl.BlockSpec(memory_space=pltpu.SMEM), hbm, vmem],
        out_specs=[hbm, vmem, vmem, vmem, vmem],
        out_shape=[
            shape(own.shape[:2] + unit, bf16),
            shape((2 * old, rows, features), bf16),
            shape((2 * old, rows, features), bf16),
            shape((2 * old, rows, inner), f32),
            shape((2 * old, rows, inner), bf16),
        ],
        scratch_shapes=[
            pltpu.VMEM((2, 2) + unit, bf16),
            pltpu.VMEM(x.shape, f32),
            pltpu.SemaphoreType.DMA((groups, 4)),
            pltpu.SemaphoreType.DMA((groups, 4)),
            pltpu.SemaphoreType.DMA((groups, deep, 9)),
            pltpu.SemaphoreType.DMA((groups, deep, 9)),
            pltpu.SemaphoreType.DMA((groups,)),
            pltpu.SemaphoreType.DMA,
        ],
        compiler_params=pltpu.CompilerParams(
            collective_id=0, has_side_effects=True, vmem_limit_bytes=48 * 2**20
        ),
        cost_estimate=pl.CostEstimate(
            flops=2 * old * rows * 8 * features * inner // 2,
            bytes_accessed=400 * 2**20,
            transcendentals=0,
        ),
    )(twice, own, x)


def wide(w):
    w = w.reshape((-1,) + w.shape[-3:])
    return jnp.concatenate([w[:, z].reshape(-1, w.shape[-1]) for z in range(w.shape[1])], axis=1)


def backward_kernel(map_ref, place_ref, g_ref, v_ref, o_ref, in_ref, pre_ref, out_g_ref, out_z_ref, state):
    @pl.when(pl.program_id(0) == 0)
    def _():
        state[...] = g_ref[...]

    g = state[...]
    gb = g.astype(bf16)
    out_g_ref[0] = gb
    gu = jnp.dot(gb, wide(o_ref[...]), preferred_element_type=f32)
    pre = pre_ref[0]
    s = jax.nn.sigmoid(pre)
    gz = (gu * s * (1.0 + pre * (1.0 - s))).astype(bf16)
    out_z_ref[0] = gz
    gh = lax.dot_general(gz, wide(v_ref[...]), (((1,), (1,)), ((), ())), preferred_element_type=f32)
    x = in_ref[0].astype(f32)
    factor = lax.rsqrt(jnp.mean(x * x, axis=-1, keepdims=True) + epsilon)
    n = x * factor
    gs = factor * (gh - n * jnp.mean(gh * n, axis=-1, keepdims=True))
    state[...] = (g + gs).astype(bf16).astype(f32)


def run_backward(layer_map, place_of, start, weights, extra):
    new = layer_map.shape[0]
    wshape = weights.shape

    def per_layer(a):
        return pl.BlockSpec((1,) + a.shape[1:], lambda j, m, p: (p[new - 1 - j], 0, 0))

    def half(which):
        def index(j, m, p):
            unit = 2 * m[new - 1 - j] + which
            return (lax.rem(unit, groups), lax.div(unit, groups), 0, 0, 0, 0)

        return pl.BlockSpec((1, 1) + wshape[2:], index)

    size = 4 * wshape[2] * wshape[3] * wshape[4] * wshape[5]
    outs = [jax.ShapeDtypeStruct((new,) + a.shape[1:], bf16) for a in extra]

    def by_layer(a):
        return pl.BlockSpec((1,) + a.shape[1:], lambda j, m, p: (new - 1 - j, 0, 0))
    return pl.pallas_call(
        backward_kernel,
        grid_spec=pltpu.PrefetchScalarGridSpec(
            num_scalar_prefetch=2,
            grid=(new,),
            in_specs=[pl.BlockSpec(start.shape, lambda j, m, p: (0, 0)), half(0), half(1)]
            + [per_layer(a) for a in extra],
            out_specs=[by_layer(a) for a in outs],
            scratch_shapes=[pltpu.VMEM(start.shape, f32)],
        ),
        out_shape=outs,
        compiler_params=pltpu.CompilerParams(
            dimension_semantics=("arbitrary",), vmem_limit_bytes=48 * 2**20
        ),
        cost_estimate=pl.CostEstimate(
            flops=new * 4 * rows * size // 4, bytes_accessed=new * size, transcendentals=0
        ),
    )(layer_map, place_of, start, weights, weights, *extra)


def pick_kernel(index_ref, keep_ref, in_ref, out_ref):
    def one(k, carry):
        kept = in_ref[index_ref[k]] * keep_ref[k].astype(f32).astype(bf16)
        out_ref[k] = kept
        return carry

    lax.fori_loop(0, out_ref.shape[0], one, 0)


def pick_slots(index, keep, pieces):
    whole = pl.BlockSpec(memory_space=pltpu.VMEM)
    scalar = pl.BlockSpec(memory_space=pltpu.SMEM)
    flat = pieces.reshape(pieces.shape[0], -1, pieces.shape[-1])
    got = pl.pallas_call(
        pick_kernel,
        in_specs=[scalar, scalar, whole],
        out_specs=whole,
        out_shape=jax.ShapeDtypeStruct((index.shape[0],) + flat.shape[1:], bf16),
        compiler_params=pltpu.CompilerParams(vmem_limit_bytes=24 * 2**20),
    )(index, keep, flat)
    return got.reshape((index.shape[0],) + pieces.shape[1:])


def pick(onehot, pieces):
    flat = pieces.reshape(pieces.shape[0], -1, pieces.shape[-1])
    got = lax.dot_general(onehot, flat, (((1,), (0,)), ((), ())), preferred_element_type=bf16)
    return got.reshape((onehot.shape[0],) + pieces.shape[1:])


def adam_update(weight, first, second, gradient, owned):
    first_new = beta_one * first + (1.0 - beta_one) * gradient
    second_new = beta_two * second + (1.0 - beta_two) * gradient * gradient
    weight_new = weight - step_rate * first_new / (jnp.sqrt(second_new) + adam_floor)
    weight_new = jnp.where(owned, weight_new, 0.0).astype(bf16)
    return (weight_new[None], first_new[None], second_new[None])


def body(
    tokens,
    cotangent,
    value_weight,
    output_weight,
    value_first,
    output_first,
    value_second,
    output_second,
    layer_map,
    old_section,
    new_section,
):
    sections = lax.axis_size(section)
    width = lax.axis_size("z")
    myself = lax.axis_index(section)
    column = lax.axis_index("z")
    new = new_section.shape[0]
    features, channels = value_weight.shape[1:]
    part = features // sections
    positions = lax.iota(jnp.int32, sections)
    owner_match = positions[:, None] == new_section[None, :]
    map_match = layer_map[:, None] == lax.iota(jnp.int32, old_section.shape[0])[None, :]
    source = jnp.sum(jnp.where(map_match, old_section[None, :], 0), axis=1)
    holds = jnp.any(owner_match, axis=1)
    wanted = jnp.sum(jnp.where(owner_match, source[None, :], 0), axis=1)
    owned = jnp.any(new_section == myself)
    my_layer = jnp.sum(jnp.where(new_section == myself, lax.iota(jnp.int32, new), 0))
    my_old = jnp.sum(jnp.where(lax.iota(jnp.int32, new) == my_layer, layer_map, 0))

    def pieces_of(arrays):
        return jnp.stack([a.reshape(sections, part, channels).astype(bf16) for a in arrays], axis=1)

    def spread(a):
        return lax.all_to_all(a, section, split_axis=0, concat_axis=0, tiled=True)

    def turned(a):
        return a.reshape(2, ring, ring, part * channels).transpose(2, 1, 0, 3)

    old = old_section.shape[0]
    pieces = spread(pieces_of((turned(value_weight), turned(output_weight))))
    deep = deep_of(2 * old)
    unit = jnp.minimum(
        groups * lax.iota(jnp.int32, deep)[None, :] + lax.iota(jnp.int32, groups)[:, None], 2 * old - 1
    ).reshape(-1)
    unit_match = (unit // 2)[:, None] == lax.iota(jnp.int32, old)[None, :]
    slots = 2 * jnp.sum(jnp.where(unit_match, old_section[None, :], 0), axis=1) + unit % 2
    own = pick_slots(slots, jnp.ones_like(slots), pieces.reshape(2 * sections, part, channels))
    count = tokens.shape[0] // sections

    def mine(a):
        block = lax.dynamic_slice_in_dim(a, myself * count, count, axis=0).astype(f32)
        return jnp.pad(block, ((0, rows - count), (0, 0)))

    numbers = lax.iota(jnp.int32, old)
    twice = (jnp.sum((layer_map[:, None] == numbers[None, :]).astype(jnp.int32), axis=0) > 1).astype(jnp.int32)
    before = jnp.concatenate([jnp.full((1,), -1, jnp.int32), layer_map[:-1]])
    place_of = 2 * layer_map + (before == layer_map).astype(jnp.int32)
    gathered, saved_in, hidden, pre, units = gather_forward(
        twice, own.reshape(groups, deep, part, channels), mine(tokens)
    )
    gathered = gathered.reshape(groups, deep, sections, width, part, channels)
    moments = pick_slots(
        wanted,
        holds.astype(jnp.int32),
        spread(pieces_of((value_first, output_first, value_second, output_second))),
    )

    send_place = jnp.sum(jnp.where(owner_match, place_of[None, :], 0), axis=1)
    places = lax.iota(jnp.int32, 2 * old)
    send_layer = ((send_place[:, None] == places[None, :]) & holds[:, None]).astype(bf16)

    def message(choice, wide, narrow):
        w = pick(choice, wide[:, :count])
        n = pick(choice, narrow[:, :count])
        n = n.reshape(sections, count, width, channels).transpose(0, 2, 1, 3)
        w = jnp.broadcast_to(w[:, None], (sections, width, count, features))
        return jnp.concatenate([w, n], axis=-1).reshape(sections * width, count, features + channels)

    def to_owner(sent):
        got = lax.all_to_all(sent, both, split_axis=0, concat_axis=0, tiled=True)
        got = got.reshape(sections * width * count, features + channels)
        return got[:, :features], got[:, features:]

    forward_sent = message(send_layer, hidden, units)
    entering = mine(cotangent)
    forward_sent, moments, entering = lax.optimization_barrier((forward_sent, moments, entering))
    hidden_all, units_all = to_owner(forward_sent)
    grads, inner_grads = run_backward(layer_map, place_of, entering, gathered, (saved_in, pre))
    grads_all, inner_all = to_owner(message(owner_match.astype(bf16), grads, inner_grads))
    moments, hidden_all = lax.optimization_barrier((moments, hidden_all))
    moments = spread(moments)

    def weight_grad(a, b):
        return lax.dot_general(a, b, (((0,), (0,)), ((), ())), preferred_element_type=f32)

    grad_value = weight_grad(hidden_all, inner_all)
    grad_output = weight_grad(grads_all, units_all)
    def own_of(which):
        unit = 2 * my_old + which
        got = lax.dynamic_slice(
            gathered,
            (unit % groups, unit // groups, 0, column, 0, 0),
            (1, 1, sections, 1, part, channels),
        )
        return got.reshape(features, channels).astype(f32)

    moments = moments.astype(f32)

    def full(a):
        return a.reshape(features, channels)

    value_new = adam_update(own_of(0), full(moments[:, 0]), full(moments[:, 2]), grad_value, owned)
    output_new = adam_update(own_of(1), full(moments[:, 1]), full(moments[:, 3]), grad_output, owned)
    return (value_new[0], output_new[0], value_new[1], output_new[1], value_new[2], output_new[2])


def solution(mesh):
    split = P(section, None, "z")
    placed = (P("z", None),) * 2 + (split,) * 6 + (P(),) * 3
    fine = Mesh(mesh.devices.reshape(ring, ring, 2, ring), both)
    return jax.shard_map(body, mesh=fine, in_specs=placed, out_specs=(split,) * 6, check_vma=False)
```

```python
import jax
import jax.numpy as jnp
from jax import lax
from jax.experimental import pallas as pl
from jax.experimental.pallas import tpu as pltpu
from jax.sharding import Mesh
from jax.sharding import PartitionSpec as P

epsilon = 1e-05
beta_one = 0.9
beta_two = 0.95
step_rate = 0.003
adam_floor = 1e-08
f32 = jnp.float32
bf16 = jnp.bfloat16
section = ("y", "x", "c")
both = ("y", "x", "c", "z")
orders = (("x", "y", "z"), ("y", "z", "x"), ("z", "x", "y"))
ring = 4
groups = 3
rows = 8
ahead = 4
early = 3
MESH = pl.DeviceIdType.MESH


def deep_of(units):
    return -(-units // groups)


def forward_layer(x, value, output):
    factor = lax.rsqrt(jnp.mean(x * x, axis=-1, keepdims=True) + epsilon)
    hidden = (x * factor).astype(bf16)
    pre = jnp.dot(hidden, value, preferred_element_type=f32)
    units = jax.nn.silu(pre).astype(bf16)
    mixing = lax.dot_general(units, output, (((1,), (1,)), ((), ())), preferred_element_type=f32)
    return (x + mixing).astype(bf16).astype(f32), hidden, pre, units


def gather_kernel(
    old,
    twice_ref,
    own_ref,
    x_ref,
    out_ref,
    in_ref,
    hid_ref,
    pre_ref,
    unit_ref,
    held,
    state,
    send_one,
    recv_one,
    send,
    recv,
    load_sem,
    own_sem,
):
    deep = deep_of(2 * old)
    me = {a: lax.axis_index(a) for a in both}

    def beside(axis, step):
        size = 2 if axis == "c" else ring
        return {axis: lax.rem(me[axis] + step + size, size)}

    barrier = pltpu.get_barrier_semaphore()
    partners = [beside(a, s) for a in ("x", "y", "z") for s in (1, -1)] + [beside("c", 1)]
    for p in partners:
        pl.semaphore_signal(barrier, inc=1, device_id=p, device_id_type=MESH)
    pl.semaphore_wait(barrier, len(partners))

    def copy(src, dst, to, send_sem, recv_sem):
        return pltpu.make_async_remote_copy(
            src_ref=src,
            dst_ref=dst,
            send_sem=send_sem,
            recv_sem=recv_sem,
            device_id=to,
            device_id_type=MESH,
        )

    def place(g, phase, k, at, half):
        full = orders[g][:phase]
        axis = orders[g][phase]
        index = dict(me)
        for a in full:
            index[a] = pl.ds(0, ring)
        if half is not None and full:
            index[full[0]] = pl.ds(half * (ring // 2), ring // 2)
        index[axis] = at
        return out_ref.at[g, k, me["c"], index["x"], index["y"], index["z"]]

    spans = ((0, early), (early, deep - early))

    def bulk_first(g, b):
        axis = orders[g][0]
        part = pl.ds(*spans[b])
        dst = place(g, 0, part, me[axis], None)
        return [
            copy(own_ref.at[g, part], dst, beside(axis, s), send_one.at[g, n], recv_one.at[g, n])
            for n, s in ((4 * b, 1), (4 * b + 1, -1))
        ]

    def bulk_second(g, b):
        axis = orders[g][0]
        lo, size = spans[b]
        cut = size // 2
        out = []
        for n, s, lo, size in ((4 * b + 2, 1, lo, cut), (4 * b + 3, -1, lo + cut, size - cut)):
            part = place(g, 0, pl.ds(lo, size), lax.rem(me[axis] - s + ring, ring), None)
            out.append(copy(part, part, beside(axis, s), send_one.at[g, n], recv_one.at[g, n]))
        return out

    def first(g, phase, k):
        axis = orders[g][phase]
        here = place(g, phase, k, me[axis], None)
        base = 4 * (phase - 1)
        return [
            copy(here, here, beside(axis, s), send.at[g, k, base + n], recv.at[g, k, base + n])
            for n, s in ((0, 1), (1, -1))
        ]

    def second(g, phase, k):
        axis = orders[g][phase]
        base = 4 * (phase - 1) + 2
        out = []
        for n, s in ((0, 1), (1, -1)):
            part = place(g, phase, k, lax.rem(me[axis] - s + ring, ring), n)
            out.append(copy(part, part, beside(axis, s), send.at[g, k, base + n], recv.at[g, k, base + n]))
        return out

    def cross(g, k):
        block = out_ref.at[g, k, me["c"]]
        return [copy(block, block, beside("c", 1), send.at[g, k, 8], recv.at[g, k, 8])]

    def start(copies):
        for c in copies:
            c.start()

    def arrived(copies):
        for c in copies:
            c.wait_recv()

    def each(k, before, after, *more):
        for g in range(groups):
            if before is not None:
                arrived(before(g, *more, k))
            start(after(g, *more, k))

    def spread_start(k):
        each(k, None, lambda g, k: first(g, 1, k))

    def spread_pass(k):
        each(k, lambda g, k: first(g, 1, k), lambda g, k: second(g, 1, k))

    def plane_start(k):
        each(k, lambda g, k: second(g, 1, k), lambda g, k: first(g, 2, k))

    def plane_pass(k):
        each(k, lambda g, k: first(g, 2, k), lambda g, k: second(g, 2, k))

    def cross_start(k):
        each(k, lambda g, k: second(g, 2, k), cross)

    def load(g, k):
        unit = groups * k + g
        layer = lax.div(unit, 2)
        return pltpu.make_async_copy(
            out_ref.at[g, k], held.at[lax.rem(layer, 2), lax.rem(unit, 2)], load_sem.at[g]
        )

    def evaluate(q, carry):
        layer = lax.div(q, 2)
        again = lax.rem(q, 2)
        slot = lax.rem(layer, 2)
        x = state[...]
        following, hidden, pre, units = forward_layer(x, wide(held[slot, 0]), wide(held[slot, 1]))
        in_ref[q] = x.astype(bf16)
        hid_ref[q] = hidden
        pre_ref[q] = pre
        unit_ref[q] = units
        keep = jnp.maximum(twice_ref[layer], 1 - again) > 0
        state[...] = jnp.where(keep, following, x)
        return carry

    def use(k):
        for g in range(groups):
            arrived(cross(g, k))
            load(g, k).start()
        for g in range(groups):
            load(g, k).wait()
        done = jnp.minimum(lax.div(groups * k + groups, 2), old)
        lax.fori_loop(2 * lax.div(groups * k, 2), 2 * done, evaluate, 0)

    mine = pltpu.make_async_copy(
        own_ref, out_ref.at[:, :, me["c"], me["x"], me["y"], me["z"]], own_sem
    )
    mine.start()
    for b in range(2):
        for g in range(groups):
            start(bulk_first(g, b))
    state[...] = x_ref[...]

    def bulk_pass(b):
        for g in range(groups):
            arrived(bulk_first(g, b))
            start(bulk_second(g, b))

    def bulk_end(b):
        for g in range(groups):
            arrived(bulk_second(g, b))

    bulk_pass(0)
    mine.wait()
    bulk_end(0)
    for k in range(early):
        spread_start(k)
    bulk_pass(1)
    spread_pass(0)
    spread_pass(1)
    plane_start(0)
    bulk_end(1)
    spread_pass(2)
    spread_start(3)
    plane_start(1)

    def step(t, carry):
        def at(k, act):
            @pl.when((k >= 0) & (k < deep))
            def _():
                act(k)

        at(t, plane_pass)
        at(t + 2, plane_start)
        at(t + 3, spread_pass)
        at(t + 4, spread_start)
        at(t - 1, cross_start)
        at(t - 2, use)
        return carry

    lax.fori_loop(0, deep + 2, step, 0)

    for g in range(groups):
        for b in range(2):
            for c in bulk_first(g, b) + bulk_second(g, b):
                c.wait_send()

    def drain(k, carry):
        for g in range(groups):
            for phase in (1, 2):
                for c in first(g, phase, k) + second(g, phase, k):
                    c.wait_send()
            for c in cross(g, k):
                c.wait_send()
        return carry

    lax.fori_loop(0, deep, drain, 0)


def gather_forward(twice, own, x):
    old = twice.shape[0]
    deep, part, channels = own.shape[-3:]
    features = x.shape[1]
    inner = ring * channels
    shape = jax.ShapeDtypeStruct
    vmem = pl.BlockSpec(memory_space=pltpu.VMEM)
    hbm = pl.BlockSpec(memory_space=pl.ANY)
    unit = (2, ring, ring, ring, part, channels)
    return pl.pallas_call(
        lambda *refs: gather_kernel(old, *refs),
        in_specs=[pl.BlockSpec(memory_space=pltpu.SMEM), hbm, vmem],
        out_specs=[hbm, vmem, vmem, vmem, vmem],
        out_shape=[
            shape(own.shape[:2] + unit, bf16),
            shape((2 * old, rows, features), bf16),
            shape((2 * old, rows, features), bf16),
            shape((2 * old, rows, inner), f32),
            shape((2 * old, rows, inner), bf16),
        ],
        scratch_shapes=[
            pltpu.VMEM((2, 2) + unit, bf16),
            pltpu.VMEM(x.shape, f32),
            pltpu.SemaphoreType.DMA((groups, 8)),
            pltpu.SemaphoreType.DMA((groups, 8)),
            pltpu.SemaphoreType.DMA((groups, deep, 9)),
            pltpu.SemaphoreType.DMA((groups, deep, 9)),
            pltpu.SemaphoreType.DMA((groups,)),
            pltpu.SemaphoreType.DMA,
        ],
        compiler_params=pltpu.CompilerParams(
            collective_id=0, has_side_effects=True, vmem_limit_bytes=48 * 2**20
        ),
        cost_estimate=pl.CostEstimate(
            flops=2 * old * rows * 8 * features * inner // 2,
            bytes_accessed=400 * 2**20,
            transcendentals=0,
        ),
    )(twice, own, x)


def wide(w):
    w = w.reshape((-1,) + w.shape[-3:])
    return jnp.concatenate([w[:, z].reshape(-1, w.shape[-1]) for z in range(w.shape[1])], axis=1)


def backward_layer(x, pre, g, value, output):
    gb = g.astype(bf16)
    gu = jnp.dot(gb, output, preferred_element_type=f32)
    s = jax.nn.sigmoid(pre)
    gz = (gu * s * (1.0 + pre * (1.0 - s))).astype(bf16)
    gh = lax.dot_general(gz, value, (((1,), (1,)), ((), ())), preferred_element_type=f32)
    factor = lax.rsqrt(jnp.mean(x * x, axis=-1, keepdims=True) + epsilon)
    n = x * factor
    gs = factor * (gh - n * jnp.mean(gh * n, axis=-1, keepdims=True))
    return (g + gs).astype(bf16).astype(f32), gb, gz


def backward_kernel(
    twice_ref, g_ref, weight_ref, in_ref, pre_ref, out_g_ref, out_z_ref, held, state, load_sem
):
    old = in_ref.shape[0] // 2
    new = out_g_ref.shape[0]

    def loads(n):
        out = []
        for h in range(2):
            unit = 2 * (old - 1 - n) + h
            slot = lax.rem(n, ahead)
            src = weight_ref.at[lax.rem(unit, groups), lax.div(unit, groups)]
            out.append(pltpu.make_async_copy(src, held.at[slot, h], load_sem.at[slot, h]))
        return out

    def start(n):
        for c in loads(n):
            c.start()

    for n in range(ahead):
        start(n)
    state[...] = g_ref[...]

    def layer(n, j):
        for c in loads(n):
            c.wait()
        slot = lax.rem(n, ahead)
        i = old - 1 - n
        extra = twice_ref[i]

        def evaluate(r, j):
            q = 2 * i + extra - r
            x = in_ref[q].astype(f32)
            g, gb, gz = backward_layer(x, pre_ref[q], state[...], wide(held[slot, 0]), wide(held[slot, 1]))
            out_g_ref[j] = gb
            out_z_ref[j] = gz
            state[...] = g
            return j - 1

        j = lax.fori_loop(0, extra + 1, evaluate, j)

        @pl.when(n + ahead < old)
        def _():
            start(n + ahead)

        return j

    lax.fori_loop(0, old, layer, new - 1)


def run_backward(new, twice, g, weights, saved_in, pre):
    shape = jax.ShapeDtypeStruct
    vmem = pl.BlockSpec(memory_space=pltpu.VMEM)
    size = 2 * weights.size // (weights.shape[0] * weights.shape[1]) * 2 * twice.shape[0]
    return pl.pallas_call(
        backward_kernel,
        in_specs=[
            pl.BlockSpec(memory_space=pltpu.SMEM),
            vmem,
            pl.BlockSpec(memory_space=pl.ANY),
            vmem,
            vmem,
        ],
        out_specs=[vmem, vmem],
        out_shape=[shape((new,) + a.shape[1:], bf16) for a in (saved_in, pre)],
        scratch_shapes=[
            pltpu.VMEM((ahead, 2) + weights.shape[2:], bf16),
            pltpu.VMEM(g.shape, f32),
            pltpu.SemaphoreType.DMA((ahead, 2)),
        ],
        compiler_params=pltpu.CompilerParams(vmem_limit_bytes=48 * 2**20),
        cost_estimate=pl.CostEstimate(
            flops=2 * rows * size, bytes_accessed=2 * size, transcendentals=0
        ),
    )(twice, g, weights, saved_in, pre)


def pick_kernel(index_ref, keep_ref, in_ref, out_ref):
    def one(k, carry):
        kept = in_ref[index_ref[k]] * keep_ref[k].astype(f32).astype(bf16)
        out_ref[k] = kept
        return carry

    lax.fori_loop(0, out_ref.shape[0], one, 0)


def pick_slots(index, keep, pieces):
    whole = pl.BlockSpec(memory_space=pltpu.VMEM)
    scalar = pl.BlockSpec(memory_space=pltpu.SMEM)
    flat = pieces.reshape(pieces.shape[0], -1, pieces.shape[-1])
    got = pl.pallas_call(
        pick_kernel,
        in_specs=[scalar, scalar, whole],
        out_specs=whole,
        out_shape=jax.ShapeDtypeStruct((index.shape[0],) + flat.shape[1:], bf16),
        compiler_params=pltpu.CompilerParams(vmem_limit_bytes=24 * 2**20),
    )(index, keep, flat)
    return got.reshape((index.shape[0],) + pieces.shape[1:])


def pick(onehot, pieces):
    flat = pieces.reshape(pieces.shape[0], -1, pieces.shape[-1])
    got = lax.dot_general(onehot, flat, (((1,), (0,)), ((), ())), preferred_element_type=bf16)
    return got.reshape((onehot.shape[0],) + pieces.shape[1:])


def adam_update(weight, first, second, gradient, owned):
    first_new = beta_one * first + (1.0 - beta_one) * gradient
    second_new = beta_two * second + (1.0 - beta_two) * gradient * gradient
    weight_new = weight - step_rate * first_new / (jnp.sqrt(second_new) + adam_floor)
    weight_new = jnp.where(owned, weight_new, 0.0).astype(bf16)
    return (weight_new[None], first_new[None], second_new[None])


def body(
    tokens,
    cotangent,
    value_weight,
    output_weight,
    value_first,
    output_first,
    value_second,
    output_second,
    layer_map,
    old_section,
    new_section,
):
    sections = lax.axis_size(section)
    width = lax.axis_size("z")
    myself = lax.axis_index(section)
    column = lax.axis_index("z")
    new = new_section.shape[0]
    features, channels = value_weight.shape[1:]
    part = features // sections
    positions = lax.iota(jnp.int32, sections)
    owner_match = positions[:, None] == new_section[None, :]
    map_match = layer_map[:, None] == lax.iota(jnp.int32, old_section.shape[0])[None, :]
    source = jnp.sum(jnp.where(map_match, old_section[None, :], 0), axis=1)
    holds = jnp.any(owner_match, axis=1)
    wanted = jnp.sum(jnp.where(owner_match, source[None, :], 0), axis=1)
    owned = jnp.any(new_section == myself)
    my_layer = jnp.sum(jnp.where(new_section == myself, lax.iota(jnp.int32, new), 0))
    my_old = jnp.sum(jnp.where(lax.iota(jnp.int32, new) == my_layer, layer_map, 0))

    def pieces_of(arrays):
        return jnp.stack([a.reshape(sections, part, channels).astype(bf16) for a in arrays], axis=1)

    def spread(a):
        return lax.all_to_all(a, section, split_axis=0, concat_axis=0, tiled=True)

    def turned(a):
        return a.reshape(2, ring, ring, part * channels).transpose(2, 1, 0, 3)

    old = old_section.shape[0]
    pieces = spread(pieces_of((turned(value_weight), turned(output_weight))))
    deep = deep_of(2 * old)
    unit = jnp.minimum(
        groups * lax.iota(jnp.int32, deep)[None, :] + lax.iota(jnp.int32, groups)[:, None], 2 * old - 1
    ).reshape(-1)
    unit_match = (unit // 2)[:, None] == lax.iota(jnp.int32, old)[None, :]
    slots = 2 * jnp.sum(jnp.where(unit_match, old_section[None, :], 0), axis=1) + unit % 2
    own = pick_slots(slots, jnp.ones_like(slots), pieces.reshape(2 * sections, part, channels))
    count = tokens.shape[0] // sections

    def mine(a):
        block = lax.dynamic_slice_in_dim(a, myself * count, count, axis=0).astype(f32)
        return jnp.pad(block, ((0, rows - count), (0, 0)))

    numbers = lax.iota(jnp.int32, old)
    twice = (jnp.sum((layer_map[:, None] == numbers[None, :]).astype(jnp.int32), axis=0) > 1).astype(jnp.int32)
    before = jnp.concatenate([jnp.full((1,), -1, jnp.int32), layer_map[:-1]])
    place_of = 2 * layer_map + (before == layer_map).astype(jnp.int32)
    gathered, saved_in, hidden, pre, units = gather_forward(
        twice, own.reshape(groups, deep, part, channels), mine(tokens)
    )
    gathered = gathered.reshape(groups, deep, sections, width, part, channels)
    moments = spread(pieces_of((value_first, output_first, value_second, output_second)))

    send_place = jnp.sum(jnp.where(owner_match, place_of[None, :], 0), axis=1)
    places = lax.iota(jnp.int32, 2 * old)
    send_layer = ((send_place[:, None] == places[None, :]) & holds[:, None]).astype(bf16)

    def message(choice, wide, narrow):
        w = pick(choice, wide[:, :count])
        n = pick(choice, narrow[:, :count])
        n = n.reshape(sections, count, width, channels).transpose(0, 2, 1, 3)
        w = jnp.broadcast_to(w[:, None], (sections, width, count, features))
        return jnp.concatenate([w, n], axis=-1).reshape(sections * width, count, features + channels)

    def to_owner(sent):
        got = lax.all_to_all(sent, both, split_axis=0, concat_axis=0, tiled=True)
        got = got.reshape(sections * width * count, features + channels)
        return got[:, :features], got[:, features:]

    forward_sent = message(send_layer, hidden, units)
    entering = mine(cotangent)
    forward_sent, moments, entering = lax.optimization_barrier((forward_sent, moments, entering))
    hidden_all, units_all = to_owner(forward_sent)
    grads, inner_grads = run_backward(new, twice, entering, gathered, saved_in, pre)
    grads_all, inner_all = to_owner(message(owner_match.astype(bf16), grads, inner_grads))
    moments, hidden_all = lax.optimization_barrier((moments, hidden_all))
    moments = pick_slots(wanted, holds.astype(jnp.int32), moments)
    moments = spread(moments)

    def weight_grad(a, b):
        return lax.dot_general(a, b, (((0,), (0,)), ((), ())), preferred_element_type=f32)

    grad_value = weight_grad(hidden_all, inner_all)
    grad_output = weight_grad(grads_all, units_all)
    def own_of(which):
        unit = 2 * my_old + which
        got = lax.dynamic_slice(
            gathered,
            (unit % groups, unit // groups, 0, column, 0, 0),
            (1, 1, sections, 1, part, channels),
        )
        return got.reshape(features, channels).astype(f32)

    moments = moments.astype(f32)

    def full(a):
        return a.reshape(features, channels)

    value_new = adam_update(own_of(0), full(moments[:, 0]), full(moments[:, 2]), grad_value, owned)
    output_new = adam_update(own_of(1), full(moments[:, 1]), full(moments[:, 3]), grad_output, owned)
    return (value_new[0], output_new[0], value_new[1], output_new[1], value_new[2], output_new[2])


def solution(mesh):
    split = P(section, None, "z")
    placed = (P("z", None),) * 2 + (split,) * 6 + (P(),) * 3
    fine = Mesh(mesh.devices.reshape(ring, ring, 2, ring), both)
    return jax.shard_map(body, mesh=fine, in_specs=placed, out_specs=(split,) * 6, check_vma=False)
```

```python
import jax
import jax.numpy as jnp
from jax import lax
from jax.experimental import pallas as pl
from jax.experimental.pallas import tpu as pltpu
from jax.sharding import Mesh
from jax.sharding import PartitionSpec as P

epsilon = 1e-05
beta_one = 0.9
beta_two = 0.95
step_rate = 0.003
adam_floor = 1e-08
f32 = jnp.float32
bf16 = jnp.bfloat16
section = ("y", "x", "c")
both = ("y", "x", "c", "z")
orders = (("x", "y", "z"), ("y", "z", "x"), ("z", "x", "y"))
ring = 4
groups = 3
rows = 8
ahead = 4
early = 3
MESH = pl.DeviceIdType.MESH


def deep_of(units):
    return -(-units // groups)


def folded(a):
    half = a.shape[1] // 2
    return (a[:, :half] + jnp.roll(a[:, half:], rows // 2, axis=0)).astype(bf16)


def repeated(a):
    return (a + jnp.roll(a, rows // 2, axis=0)).astype(bf16)


def forward_layer(x, value, output):
    factor = lax.rsqrt(jnp.mean(x * x, axis=-1, keepdims=True) + epsilon)
    hidden = (x * factor).astype(bf16)
    pre = jnp.dot(hidden, value, preferred_element_type=f32)
    units = jax.nn.silu(pre).astype(bf16)
    mixing = lax.dot_general(units, output, (((1,), (1,)), ((), ())), preferred_element_type=f32)
    return (x + mixing).astype(bf16).astype(f32), hidden, pre, units


def gather_kernel(
    old,
    twice_ref,
    own_ref,
    x_ref,
    out_ref,
    in_ref,
    hid_ref,
    pre_ref,
    unit_ref,
    held,
    state,
    send_one,
    recv_one,
    send,
    recv,
    load_sem,
    own_sem,
):
    deep = deep_of(2 * old)
    me = {a: lax.axis_index(a) for a in both}

    def beside(axis, step):
        size = 2 if axis == "c" else ring
        return {axis: lax.rem(me[axis] + step + size, size)}

    barrier = pltpu.get_barrier_semaphore()
    partners = [beside(a, s) for a in ("x", "y", "z") for s in (1, -1)] + [beside("c", 1)]
    for p in partners:
        pl.semaphore_signal(barrier, inc=1, device_id=p, device_id_type=MESH)
    pl.semaphore_wait(barrier, len(partners))

    def copy(src, dst, to, send_sem, recv_sem):
        return pltpu.make_async_remote_copy(
            src_ref=src,
            dst_ref=dst,
            send_sem=send_sem,
            recv_sem=recv_sem,
            device_id=to,
            device_id_type=MESH,
        )

    def place(g, phase, k, at, half):
        full = orders[g][:phase]
        axis = orders[g][phase]
        index = dict(me)
        for a in full:
            index[a] = pl.ds(0, ring)
        if half is not None and full:
            index[full[0]] = pl.ds(half * (ring // 2), ring // 2)
        index[axis] = at
        return out_ref.at[g, k, me["c"], index["x"], index["y"], index["z"]]

    spans = ((0, early), (early, deep - early))

    def bulk_first(g, b):
        axis = orders[g][0]
        part = pl.ds(*spans[b])
        dst = place(g, 0, part, me[axis], None)
        return [
            copy(own_ref.at[g, part], dst, beside(axis, s), send_one.at[g, n], recv_one.at[g, n])
            for n, s in ((4 * b, 1), (4 * b + 1, -1))
        ]

    def bulk_second(g, b):
        axis = orders[g][0]
        lo, size = spans[b]
        cut = size // 2
        out = []
        for n, s, lo, size in ((4 * b + 2, 1, lo, cut), (4 * b + 3, -1, lo + cut, size - cut)):
            part = place(g, 0, pl.ds(lo, size), lax.rem(me[axis] - s + ring, ring), None)
            out.append(copy(part, part, beside(axis, s), send_one.at[g, n], recv_one.at[g, n]))
        return out

    def first(g, phase, k):
        axis = orders[g][phase]
        here = place(g, phase, k, me[axis], None)
        base = 4 * (phase - 1)
        return [
            copy(here, here, beside(axis, s), send.at[g, k, base + n], recv.at[g, k, base + n])
            for n, s in ((0, 1), (1, -1))
        ]

    def second(g, phase, k):
        axis = orders[g][phase]
        base = 4 * (phase - 1) + 2
        out = []
        for n, s in ((0, 1), (1, -1)):
            part = place(g, phase, k, lax.rem(me[axis] - s + ring, ring), n)
            out.append(copy(part, part, beside(axis, s), send.at[g, k, base + n], recv.at[g, k, base + n]))
        return out

    def cross(g, k):
        block = out_ref.at[g, k, me["c"]]
        return [copy(block, block, beside("c", 1), send.at[g, k, 8], recv.at[g, k, 8])]

    def start(copies):
        for c in copies:
            c.start()

    def arrived(copies):
        for c in copies:
            c.wait_recv()

    def each(k, before, after, *more):
        for g in range(groups):
            if before is not None:
                arrived(before(g, *more, k))
            start(after(g, *more, k))

    def spread_start(k):
        each(k, None, lambda g, k: first(g, 1, k))

    def spread_pass(k):
        each(k, lambda g, k: first(g, 1, k), lambda g, k: second(g, 1, k))

    def plane_start(k):
        each(k, lambda g, k: second(g, 1, k), lambda g, k: first(g, 2, k))

    def plane_pass(k):
        each(k, lambda g, k: first(g, 2, k), lambda g, k: second(g, 2, k))

    def cross_start(k):
        each(k, lambda g, k: second(g, 2, k), cross)

    def load(g, k):
        unit = groups * k + g
        layer = lax.div(unit, 2)
        return pltpu.make_async_copy(
            out_ref.at[g, k], held.at[lax.rem(layer, 2), lax.rem(unit, 2)], load_sem.at[g]
        )

    def evaluate(q, carry):
        layer = lax.div(q, 2)
        again = lax.rem(q, 2)
        slot = lax.rem(layer, 2)
        x = state[...]
        following, hidden, pre, units = forward_layer(x, wide(held[slot, 0]), wide(held[slot, 1]))
        in_ref[q] = x.astype(bf16)
        hid_ref[q] = folded(hidden.astype(f32))
        pre_ref[q] = pre
        unit_ref[q] = repeated(units.astype(f32))
        keep = jnp.maximum(twice_ref[layer], 1 - again) > 0
        state[...] = jnp.where(keep, following, x)
        return carry

    def use(k):
        for g in range(groups):
            arrived(cross(g, k))
            load(g, k).start()
        for g in range(groups):
            load(g, k).wait()
        done = jnp.minimum(lax.div(groups * k + groups, 2), old)
        lax.fori_loop(2 * lax.div(groups * k, 2), 2 * done, evaluate, 0)

    mine = pltpu.make_async_copy(
        own_ref, out_ref.at[:, :, me["c"], me["x"], me["y"], me["z"]], own_sem
    )
    mine.start()
    for b in range(2):
        for g in range(groups):
            start(bulk_first(g, b))
    state[...] = x_ref[...]

    def bulk_pass(b):
        for g in range(groups):
            arrived(bulk_first(g, b))
            start(bulk_second(g, b))

    def bulk_end(b):
        for g in range(groups):
            arrived(bulk_second(g, b))

    bulk_pass(0)
    mine.wait()
    bulk_end(0)
    for k in range(early):
        spread_start(k)
    bulk_pass(1)
    spread_pass(0)
    spread_pass(1)
    plane_start(0)
    bulk_end(1)
    spread_pass(2)
    spread_start(3)
    plane_start(1)

    def step(t, carry):
        def at(k, act):
            @pl.when((k >= 0) & (k < deep))
            def _():
                act(k)

        at(t, plane_pass)
        at(t + 2, plane_start)
        at(t + 3, spread_pass)
        at(t + 4, spread_start)
        at(t - 1, cross_start)
        at(t - 2, use)
        return carry

    lax.fori_loop(0, deep + 2, step, 0)

    for g in range(groups):
        for b in range(2):
            for c in bulk_first(g, b) + bulk_second(g, b):
                c.wait_send()

    def drain(k, carry):
        for g in range(groups):
            for phase in (1, 2):
                for c in first(g, phase, k) + second(g, phase, k):
                    c.wait_send()
            for c in cross(g, k):
                c.wait_send()
        return carry

    lax.fori_loop(0, deep, drain, 0)


def gather_forward(twice, own, x):
    old = twice.shape[0]
    deep, part, channels = own.shape[-3:]
    features = x.shape[1]
    inner = ring * channels
    shape = jax.ShapeDtypeStruct
    vmem = pl.BlockSpec(memory_space=pltpu.VMEM)
    hbm = pl.BlockSpec(memory_space=pl.ANY)
    unit = (2, ring, ring, ring, part, channels)
    return pl.pallas_call(
        lambda *refs: gather_kernel(old, *refs),
        in_specs=[pl.BlockSpec(memory_space=pltpu.SMEM), hbm, vmem],
        out_specs=[hbm, vmem, vmem, vmem, vmem],
        out_shape=[
            shape(own.shape[:2] + unit, bf16),
            shape((2 * old, rows, features), bf16),
            shape((2 * old, rows, features // 2), bf16),
            shape((2 * old, rows, inner), f32),
            shape((2 * old, rows, inner), bf16),
        ],
        scratch_shapes=[
            pltpu.VMEM((2, 2) + unit, bf16),
            pltpu.VMEM(x.shape, f32),
            pltpu.SemaphoreType.DMA((groups, 8)),
            pltpu.SemaphoreType.DMA((groups, 8)),
            pltpu.SemaphoreType.DMA((groups, deep, 9)),
            pltpu.SemaphoreType.DMA((groups, deep, 9)),
            pltpu.SemaphoreType.DMA((groups,)),
            pltpu.SemaphoreType.DMA,
        ],
        compiler_params=pltpu.CompilerParams(
            collective_id=0, has_side_effects=True, vmem_limit_bytes=48 * 2**20
        ),
        cost_estimate=pl.CostEstimate(
            flops=2 * old * rows * 8 * features * inner // 2,
            bytes_accessed=400 * 2**20,
            transcendentals=0,
        ),
    )(twice, own, x)


def wide(w):
    w = w.reshape((-1,) + w.shape[-3:])
    return jnp.concatenate([w[:, z].reshape(-1, w.shape[-1]) for z in range(w.shape[1])], axis=1)


def backward_layer(x, pre, g, value, output):
    gb = g.astype(bf16)
    gu = jnp.dot(gb, output, preferred_element_type=f32)
    s = jax.nn.sigmoid(pre)
    gz = (gu * s * (1.0 + pre * (1.0 - s))).astype(bf16)
    gh = lax.dot_general(gz, value, (((1,), (1,)), ((), ())), preferred_element_type=f32)
    factor = lax.rsqrt(jnp.mean(x * x, axis=-1, keepdims=True) + epsilon)
    n = x * factor
    gs = factor * (gh - n * jnp.mean(gh * n, axis=-1, keepdims=True))
    return (g + gs).astype(bf16).astype(f32), gb, gz


def backward_kernel(
    twice_ref, g_ref, weight_ref, in_ref, pre_ref, out_g_ref, out_z_ref, held, state, load_sem
):
    old = in_ref.shape[0] // 2
    new = out_g_ref.shape[0]

    def loads(n):
        out = []
        for h in range(2):
            unit = 2 * (old - 1 - n) + h
            slot = lax.rem(n, ahead)
            src = weight_ref.at[lax.rem(unit, groups), lax.div(unit, groups)]
            out.append(pltpu.make_async_copy(src, held.at[slot, h], load_sem.at[slot, h]))
        return out

    def start(n):
        for c in loads(n):
            c.start()

    for n in range(ahead):
        start(n)
    state[...] = g_ref[...]

    def layer(n, j):
        for c in loads(n):
            c.wait()
        slot = lax.rem(n, ahead)
        i = old - 1 - n
        extra = twice_ref[i]

        def evaluate(r, j):
            q = 2 * i + extra - r
            x = in_ref[q].astype(f32)
            g, gb, gz = backward_layer(x, pre_ref[q], state[...], wide(held[slot, 0]), wide(held[slot, 1]))
            out_g_ref[j] = folded(gb.astype(f32))
            out_z_ref[j] = repeated(gz.astype(f32))
            state[...] = g
            return j - 1

        j = lax.fori_loop(0, extra + 1, evaluate, j)

        @pl.when(n + ahead < old)
        def _():
            start(n + ahead)

        return j

    lax.fori_loop(0, old, layer, new - 1)


def run_backward(new, twice, g, weights, saved_in, pre):
    shape = jax.ShapeDtypeStruct
    vmem = pl.BlockSpec(memory_space=pltpu.VMEM)
    size = 2 * weights.size // (weights.shape[0] * weights.shape[1]) * 2 * twice.shape[0]
    return pl.pallas_call(
        backward_kernel,
        in_specs=[
            pl.BlockSpec(memory_space=pltpu.SMEM),
            vmem,
            pl.BlockSpec(memory_space=pl.ANY),
            vmem,
            vmem,
        ],
        out_specs=[vmem, vmem],
        out_shape=[
            shape((new, rows, saved_in.shape[2] // 2), bf16),
            shape((new, rows, pre.shape[2]), bf16),
        ],
        scratch_shapes=[
            pltpu.VMEM((ahead, 2) + weights.shape[2:], bf16),
            pltpu.VMEM(g.shape, f32),
            pltpu.SemaphoreType.DMA((ahead, 2)),
        ],
        compiler_params=pltpu.CompilerParams(vmem_limit_bytes=48 * 2**20),
        cost_estimate=pl.CostEstimate(
            flops=2 * rows * size, bytes_accessed=2 * size, transcendentals=0
        ),
    )(twice, g, weights, saved_in, pre)


def pick_kernel(index_ref, keep_ref, in_ref, out_ref):
    def one(k, carry):
        kept = in_ref[index_ref[k]] * keep_ref[k].astype(f32).astype(bf16)
        out_ref[k] = kept
        return carry

    lax.fori_loop(0, out_ref.shape[0], one, 0)


def pick_slots(index, keep, pieces):
    whole = pl.BlockSpec(memory_space=pltpu.VMEM)
    scalar = pl.BlockSpec(memory_space=pltpu.SMEM)
    flat = pieces.reshape(pieces.shape[0], -1, pieces.shape[-1])
    got = pl.pallas_call(
        pick_kernel,
        in_specs=[scalar, scalar, whole],
        out_specs=whole,
        out_shape=jax.ShapeDtypeStruct((index.shape[0],) + flat.shape[1:], bf16),
        compiler_params=pltpu.CompilerParams(vmem_limit_bytes=24 * 2**20),
    )(index, keep, flat)
    return got.reshape((index.shape[0],) + pieces.shape[1:])


def pick(onehot, pieces):
    flat = pieces.reshape(pieces.shape[0], -1, pieces.shape[-1])
    got = lax.dot_general(onehot, flat, (((1,), (0,)), ((), ())), preferred_element_type=bf16)
    return got.reshape((onehot.shape[0],) + pieces.shape[1:])


def adam_update(weight, first, second, gradient, owned):
    first_new = beta_one * first + (1.0 - beta_one) * gradient
    second_new = beta_two * second + (1.0 - beta_two) * gradient * gradient
    weight_new = weight - step_rate * first_new / (jnp.sqrt(second_new) + adam_floor)
    weight_new = jnp.where(owned, weight_new, 0.0).astype(bf16)
    return (weight_new[None], first_new[None], second_new[None])


def body(
    tokens,
    cotangent,
    value_weight,
    output_weight,
    value_first,
    output_first,
    value_second,
    output_second,
    layer_map,
    old_section,
    new_section,
):
    sections = lax.axis_size(section)
    width = lax.axis_size("z")
    myself = lax.axis_index(section)
    column = lax.axis_index("z")
    new = new_section.shape[0]
    features, channels = value_weight.shape[1:]
    part = features // sections
    positions = lax.iota(jnp.int32, sections)
    owner_match = positions[:, None] == new_section[None, :]
    map_match = layer_map[:, None] == lax.iota(jnp.int32, old_section.shape[0])[None, :]
    source = jnp.sum(jnp.where(map_match, old_section[None, :], 0), axis=1)
    holds = jnp.any(owner_match, axis=1)
    wanted = jnp.sum(jnp.where(owner_match, source[None, :], 0), axis=1)
    owned = jnp.any(new_section == myself)
    my_layer = jnp.sum(jnp.where(new_section == myself, lax.iota(jnp.int32, new), 0))
    my_old = jnp.sum(jnp.where(lax.iota(jnp.int32, new) == my_layer, layer_map, 0))

    def pieces_of(arrays):
        return jnp.stack([a.reshape(sections, part, channels).astype(bf16) for a in arrays], axis=1)

    def spread(a):
        return lax.all_to_all(a, section, split_axis=0, concat_axis=0, tiled=True)

    def turned(a):
        return a.reshape(2, ring, ring, part * channels).transpose(2, 1, 0, 3)

    old = old_section.shape[0]
    pieces = spread(pieces_of((turned(value_weight), turned(output_weight))))
    deep = deep_of(2 * old)
    unit = jnp.minimum(
        groups * lax.iota(jnp.int32, deep)[None, :] + lax.iota(jnp.int32, groups)[:, None], 2 * old - 1
    ).reshape(-1)
    unit_match = (unit // 2)[:, None] == lax.iota(jnp.int32, old)[None, :]
    slots = 2 * jnp.sum(jnp.where(unit_match, old_section[None, :], 0), axis=1) + unit % 2
    own = pick_slots(slots, jnp.ones_like(slots), pieces.reshape(2 * sections, part, channels))
    count = tokens.shape[0] // sections

    def mine(a):
        block = lax.dynamic_slice_in_dim(a, myself * count, count, axis=0).astype(f32)
        return jnp.pad(block, ((0, rows - count), (0, 0)))

    numbers = lax.iota(jnp.int32, old)
    twice = (jnp.sum((layer_map[:, None] == numbers[None, :]).astype(jnp.int32), axis=0) > 1).astype(jnp.int32)
    before = jnp.concatenate([jnp.full((1,), -1, jnp.int32), layer_map[:-1]])
    place_of = 2 * layer_map + (before == layer_map).astype(jnp.int32)
    gathered, saved_in, hidden, pre, units = gather_forward(
        twice, own.reshape(groups, deep, part, channels), mine(tokens)
    )
    gathered = gathered.reshape(groups, deep, sections, width, part, channels)
    moments = spread(pieces_of((value_first, output_first, value_second, output_second)))

    send_place = jnp.sum(jnp.where(owner_match, place_of[None, :], 0), axis=1)
    places = lax.iota(jnp.int32, 2 * old)
    send_layer = ((send_place[:, None] == places[None, :]) & holds[:, None]).astype(bf16)

    def message(choice, wide, narrow):
        w = pick(choice, wide)
        n = pick(choice, narrow)
        n = n.reshape(sections, rows, width, channels).transpose(0, 2, 1, 3)
        w = jnp.broadcast_to(w[:, None], (sections, width) + w.shape[1:])
        return [w, n]

    entering = mine(cotangent)
    moments, saved_in = lax.optimization_barrier((moments, saved_in))
    moments = pick_slots(wanted, holds.astype(jnp.int32), moments)
    moments, entering = lax.optimization_barrier((moments, entering))
    moments = spread(moments)
    grads, inner_grads = run_backward(new, twice, entering, gathered, saved_in, pre)
    sent = message(send_layer, hidden, units) + message(owner_match.astype(bf16), grads, inner_grads)
    sent = jnp.concatenate(sent, axis=-1)
    sent = sent.reshape((sections * width,) + sent.shape[2:])
    got = lax.all_to_all(sent, both, split_axis=0, concat_axis=0, tiled=True)
    got = got.reshape(sections * width * rows, got.shape[-1])
    fold = features // 2
    low = (lax.broadcasted_iota(jnp.int32, (got.shape[0], 1), 0) % rows) < rows // 2

    def weight_grad(a, b):
        b = jnp.concatenate([jnp.where(low, b, 0), jnp.where(low, 0, b)], axis=1)
        g = lax.dot_general(a, b, (((0,), (0,)), ((), ())), preferred_element_type=f32)
        return jnp.concatenate([g[:, :channels], g[:, channels:]], axis=0)

    grad_value = weight_grad(got[:, :fold], got[:, 2 * fold + channels :])
    grad_output = weight_grad(got[:, fold + channels : 2 * fold + channels], got[:, fold : fold + channels])

    def own_of(which):
        unit = 2 * my_old + which
        got = lax.dynamic_slice(
            gathered,
            (unit % groups, unit // groups, 0, column, 0, 0),
            (1, 1, sections, 1, part, channels),
        )
        return got.reshape(features, channels).astype(f32)

    moments = moments.astype(f32)

    def full(a):
        return a.reshape(features, channels)

    value_new = adam_update(own_of(0), full(moments[:, 0]), full(moments[:, 2]), grad_value, owned)
    output_new = adam_update(own_of(1), full(moments[:, 1]), full(moments[:, 3]), grad_output, owned)
    return (value_new[0], output_new[0], value_new[1], output_new[1], value_new[2], output_new[2])


def solution(mesh):
    split = P(section, None, "z")
    placed = (P("z", None),) * 2 + (split,) * 6 + (P(),) * 3
    fine = Mesh(mesh.devices.reshape(ring, ring, 2, ring), both)
    return jax.shard_map(body, mesh=fine, in_specs=placed, out_specs=(split,) * 6, check_vma=False)
```

```python
import jax
import jax.numpy as jnp
from jax import lax
from jax.experimental import pallas as pl
from jax.experimental.pallas import tpu as pltpu
from jax.sharding import Mesh
from jax.sharding import PartitionSpec as P

epsilon = 1e-05
beta_one = 0.9
beta_two = 0.95
step_rate = 0.003
adam_floor = 1e-08
f32 = jnp.float32
bf16 = jnp.bfloat16
section = ("y", "x", "c")
both = ("y", "x", "c", "z")
orders = (("x", "y", "z"), ("y", "z", "x"), ("z", "x", "y"))
ring = 4
groups = 3
rows = 8
ahead = 4
early = 3
MESH = pl.DeviceIdType.MESH


def deep_of(units):
    return -(-units // groups)


def folded(a):
    half = a.shape[1] // 2
    return (a[:, :half] + jnp.roll(a[:, half:], rows // 2, axis=0)).astype(bf16)


def repeated(a):
    return (a + jnp.roll(a, rows // 2, axis=0)).astype(bf16)


def forward_layer(x, value, output):
    factor = lax.rsqrt(jnp.mean(x * x, axis=-1, keepdims=True) + epsilon)
    hidden = (x * factor).astype(bf16)
    pre = jnp.dot(hidden, value, preferred_element_type=f32)
    units = jax.nn.silu(pre).astype(bf16)
    mixing = lax.dot_general(units, output, (((1,), (1,)), ((), ())), preferred_element_type=f32)
    return (x + mixing).astype(bf16).astype(f32), hidden, pre, units


def gather_kernel(
    old,
    twice_ref,
    own_ref,
    x_ref,
    out_ref,
    in_ref,
    hid_ref,
    pre_ref,
    unit_ref,
    held,
    state,
    send_one,
    recv_one,
    send,
    recv,
    load_sem,
    own_sem,
):
    deep = deep_of(2 * old)
    me = {a: lax.axis_index(a) for a in both}

    def beside(axis, step):
        size = 2 if axis == "c" else ring
        return {axis: lax.rem(me[axis] + step + size, size)}

    barrier = pltpu.get_barrier_semaphore()
    partners = [beside(a, s) for a in ("x", "y", "z") for s in (1, -1)] + [beside("c", 1)]
    for p in partners:
        pl.semaphore_signal(barrier, inc=1, device_id=p, device_id_type=MESH)
    pl.semaphore_wait(barrier, len(partners))

    def copy(src, dst, to, send_sem, recv_sem):
        return pltpu.make_async_remote_copy(
            src_ref=src,
            dst_ref=dst,
            send_sem=send_sem,
            recv_sem=recv_sem,
            device_id=to,
            device_id_type=MESH,
        )

    def place(g, phase, k, at, half):
        full = orders[g][:phase]
        axis = orders[g][phase]
        index = dict(me)
        for a in full:
            index[a] = pl.ds(0, ring)
        if half is not None and full:
            index[full[0]] = pl.ds(half * (ring // 2), ring // 2)
        index[axis] = at
        return out_ref.at[g, k, me["c"], index["x"], index["y"], index["z"]]

    spans = ((0, early), (early, deep - early))

    def bulk_first(g, b):
        axis = orders[g][0]
        part = pl.ds(*spans[b])
        dst = place(g, 0, part, me[axis], None)
        return [
            copy(own_ref.at[g, part], dst, beside(axis, s), send_one.at[g, n], recv_one.at[g, n])
            for n, s in ((4 * b, 1), (4 * b + 1, -1))
        ]

    def bulk_second(g, b):
        axis = orders[g][0]
        lo, size = spans[b]
        cut = size // 2
        out = []
        for n, s, lo, size in ((4 * b + 2, 1, lo, cut), (4 * b + 3, -1, lo + cut, size - cut)):
            part = place(g, 0, pl.ds(lo, size), lax.rem(me[axis] - s + ring, ring), None)
            out.append(copy(part, part, beside(axis, s), send_one.at[g, n], recv_one.at[g, n]))
        return out

    def first(g, phase, k):
        axis = orders[g][phase]
        here = place(g, phase, k, me[axis], None)
        base = 4 * (phase - 1)
        return [
            copy(here, here, beside(axis, s), send.at[g, k, base + n], recv.at[g, k, base + n])
            for n, s in ((0, 1), (1, -1))
        ]

    def second(g, phase, k):
        axis = orders[g][phase]
        base = 4 * (phase - 1) + 2
        out = []
        for n, s in ((0, 1), (1, -1)):
            part = place(g, phase, k, lax.rem(me[axis] - s + ring, ring), n)
            out.append(copy(part, part, beside(axis, s), send.at[g, k, base + n], recv.at[g, k, base + n]))
        return out

    def cross(g, k):
        block = out_ref.at[g, k, me["c"]]
        return [copy(block, block, beside("c", 1), send.at[g, k, 8], recv.at[g, k, 8])]

    def start(copies):
        for c in copies:
            c.start()

    def arrived(copies):
        for c in copies:
            c.wait_recv()

    def each(k, before, after, *more):
        for g in range(groups):
            if before is not None:
                arrived(before(g, *more, k))
            start(after(g, *more, k))

    def spread_start(k):
        each(k, None, lambda g, k: first(g, 1, k))

    def spread_pass(k):
        each(k, lambda g, k: first(g, 1, k), lambda g, k: second(g, 1, k))

    def plane_start(k):
        each(k, lambda g, k: second(g, 1, k), lambda g, k: first(g, 2, k))

    def plane_pass(k):
        each(k, lambda g, k: first(g, 2, k), lambda g, k: second(g, 2, k))

    def cross_start(k):
        each(k, lambda g, k: second(g, 2, k), cross)

    def load(g, k):
        unit = groups * k + g
        layer = lax.div(unit, 2)
        return pltpu.make_async_copy(
            out_ref.at[g, k], held.at[lax.rem(layer, 2), lax.rem(unit, 2)], load_sem.at[g]
        )

    def evaluate(q, carry):
        layer = lax.div(q, 2)
        again = lax.rem(q, 2)
        slot = lax.rem(layer, 2)
        x = state[...]
        following, hidden, pre, units = forward_layer(x, wide(held[slot, 0]), wide(held[slot, 1]))
        in_ref[q] = x.astype(bf16)
        hid_ref[q] = folded(hidden.astype(f32))
        pre_ref[q] = pre
        unit_ref[q] = repeated(units.astype(f32))
        keep = jnp.maximum(twice_ref[layer], 1 - again) > 0
        state[...] = jnp.where(keep, following, x)
        return carry

    def use(k):
        for g in range(groups):
            arrived(cross(g, k))
            load(g, k).start()
        for g in range(groups):
            load(g, k).wait()
        done = jnp.minimum(lax.div(groups * k + groups, 2), old)
        lax.fori_loop(2 * lax.div(groups * k, 2), 2 * done, evaluate, 0)

    mine = pltpu.make_async_copy(
        own_ref, out_ref.at[:, :, me["c"], me["x"], me["y"], me["z"]], own_sem
    )
    mine.start()
    for b in range(2):
        for g in range(groups):
            start(bulk_first(g, b))
    state[...] = x_ref[...]

    def bulk_pass(b):
        for g in range(groups):
            arrived(bulk_first(g, b))
            start(bulk_second(g, b))

    def bulk_end(b):
        for g in range(groups):
            arrived(bulk_second(g, b))

    bulk_pass(0)
    mine.wait()
    bulk_end(0)
    for k in range(early):
        spread_start(k)
    bulk_pass(1)
    spread_pass(0)
    spread_pass(1)
    plane_start(0)
    bulk_end(1)
    spread_pass(2)
    spread_start(3)
    plane_start(1)

    def drain(k):
        for g in range(groups):
            for phase in (1, 2):
                for c in first(g, phase, k) + second(g, phase, k):
                    c.wait_send()
            for c in cross(g, k):
                c.wait_send()

    def step(t, carry):
        def at(k, act):
            @pl.when((k >= 0) & (k < deep))
            def _():
                act(k)

        at(t, plane_pass)
        at(t + 2, plane_start)
        at(t + 3, spread_pass)
        at(t + 4, spread_start)
        at(t - 1, cross_start)
        at(t - 2, use)
        at(t - 3, drain)

        @pl.when(t == 1)
        def _():
            for g in range(groups):
                for b in range(2):
                    for c in bulk_first(g, b) + bulk_second(g, b):
                        c.wait_send()

        return carry

    lax.fori_loop(0, deep + 2, step, 0)
    drain(deep - 1)


def gather_forward(twice, own, x):
    old = twice.shape[0]
    deep, part, channels = own.shape[-3:]
    features = x.shape[1]
    inner = ring * channels
    shape = jax.ShapeDtypeStruct
    vmem = pl.BlockSpec(memory_space=pltpu.VMEM)
    hbm = pl.BlockSpec(memory_space=pl.ANY)
    unit = (2, ring, ring, ring, part, channels)
    return pl.pallas_call(
        lambda *refs: gather_kernel(old, *refs),
        in_specs=[pl.BlockSpec(memory_space=pltpu.SMEM), hbm, vmem],
        out_specs=[hbm, vmem, vmem, vmem, vmem],
        out_shape=[
            shape(own.shape[:2] + unit, bf16),
            shape((2 * old, rows, features), bf16),
            shape((2 * old, rows, features // 2), bf16),
            shape((2 * old, rows, inner), f32),
            shape((2 * old, rows, inner), bf16),
        ],
        scratch_shapes=[
            pltpu.VMEM((2, 2) + unit, bf16),
            pltpu.VMEM(x.shape, f32),
            pltpu.SemaphoreType.DMA((groups, 8)),
            pltpu.SemaphoreType.DMA((groups, 8)),
            pltpu.SemaphoreType.DMA((groups, deep, 9)),
            pltpu.SemaphoreType.DMA((groups, deep, 9)),
            pltpu.SemaphoreType.DMA((groups,)),
            pltpu.SemaphoreType.DMA,
        ],
        compiler_params=pltpu.CompilerParams(
            collective_id=0, has_side_effects=True, vmem_limit_bytes=48 * 2**20
        ),
        cost_estimate=pl.CostEstimate(
            flops=2 * old * rows * 8 * features * inner // 2,
            bytes_accessed=400 * 2**20,
            transcendentals=0,
        ),
    )(twice, own, x)


def wide(w):
    w = w.reshape((-1,) + w.shape[-3:])
    return jnp.concatenate([w[:, z].reshape(-1, w.shape[-1]) for z in range(w.shape[1])], axis=1)


def backward_layer(x, pre, g, value, output):
    gb = g.astype(bf16)
    gu = jnp.dot(gb, output, preferred_element_type=f32)
    s = jax.nn.sigmoid(pre)
    gz = (gu * s * (1.0 + pre * (1.0 - s))).astype(bf16)
    gh = lax.dot_general(gz, value, (((1,), (1,)), ((), ())), preferred_element_type=f32)
    factor = lax.rsqrt(jnp.mean(x * x, axis=-1, keepdims=True) + epsilon)
    n = x * factor
    gs = factor * (gh - n * jnp.mean(gh * n, axis=-1, keepdims=True))
    return (g + gs).astype(bf16).astype(f32), gb, gz


def backward_kernel(
    twice_ref, g_ref, weight_ref, in_ref, pre_ref, out_g_ref, out_z_ref, held, state, load_sem
):
    old = in_ref.shape[0] // 2
    new = out_g_ref.shape[0]

    def loads(n):
        out = []
        for h in range(2):
            unit = 2 * (old - 1 - n) + h
            slot = lax.rem(n, ahead)
            src = weight_ref.at[lax.rem(unit, groups), lax.div(unit, groups)]
            out.append(pltpu.make_async_copy(src, held.at[slot, h], load_sem.at[slot, h]))
        return out

    def start(n):
        for c in loads(n):
            c.start()

    for n in range(ahead):
        start(n)
    state[...] = g_ref[...]

    def layer(n, j):
        for c in loads(n):
            c.wait()
        slot = lax.rem(n, ahead)
        i = old - 1 - n
        extra = twice_ref[i]

        def evaluate(r, j):
            q = 2 * i + extra - r
            x = in_ref[q].astype(f32)
            g, gb, gz = backward_layer(x, pre_ref[q], state[...], wide(held[slot, 0]), wide(held[slot, 1]))
            out_g_ref[j] = folded(gb.astype(f32))
            out_z_ref[j] = repeated(gz.astype(f32))
            state[...] = g
            return j - 1

        j = lax.fori_loop(0, extra + 1, evaluate, j)

        @pl.when(n + ahead < old)
        def _():
            start(n + ahead)

        return j

    lax.fori_loop(0, old, layer, new - 1)


def run_backward(new, twice, g, weights, saved_in, pre):
    shape = jax.ShapeDtypeStruct
    vmem = pl.BlockSpec(memory_space=pltpu.VMEM)
    size = 2 * weights.size // (weights.shape[0] * weights.shape[1]) * 2 * twice.shape[0]
    return pl.pallas_call(
        backward_kernel,
        in_specs=[
            pl.BlockSpec(memory_space=pltpu.SMEM),
            vmem,
            pl.BlockSpec(memory_space=pl.ANY),
            vmem,
            vmem,
        ],
        out_specs=[vmem, vmem],
        out_shape=[
            shape((new, rows, saved_in.shape[2] // 2), bf16),
            shape((new, rows, pre.shape[2]), bf16),
        ],
        scratch_shapes=[
            pltpu.VMEM((ahead, 2) + weights.shape[2:], bf16),
            pltpu.VMEM(g.shape, f32),
            pltpu.SemaphoreType.DMA((ahead, 2)),
        ],
        compiler_params=pltpu.CompilerParams(vmem_limit_bytes=48 * 2**20),
        cost_estimate=pl.CostEstimate(
            flops=2 * rows * size, bytes_accessed=2 * size, transcendentals=0
        ),
    )(twice, g, weights, saved_in, pre)


def pick_kernel(index_ref, keep_ref, in_ref, out_ref):
    def one(k, carry):
        kept = in_ref[index_ref[k]] * keep_ref[k].astype(f32).astype(bf16)
        out_ref[k] = kept
        return carry

    lax.fori_loop(0, out_ref.shape[0], one, 0)


def pick_slots(index, keep, pieces):
    whole = pl.BlockSpec(memory_space=pltpu.VMEM)
    scalar = pl.BlockSpec(memory_space=pltpu.SMEM)
    flat = pieces.reshape(pieces.shape[0], -1, pieces.shape[-1])
    got = pl.pallas_call(
        pick_kernel,
        in_specs=[scalar, scalar, whole],
        out_specs=whole,
        out_shape=jax.ShapeDtypeStruct((index.shape[0],) + flat.shape[1:], bf16),
        compiler_params=pltpu.CompilerParams(vmem_limit_bytes=24 * 2**20),
    )(index, keep, flat)
    return got.reshape((index.shape[0],) + pieces.shape[1:])


def pick(onehot, pieces):
    flat = pieces.reshape(pieces.shape[0], -1, pieces.shape[-1])
    got = lax.dot_general(onehot, flat, (((1,), (0,)), ((), ())), preferred_element_type=bf16)
    return got.reshape((onehot.shape[0],) + pieces.shape[1:])


def adam_update(weight, first, second, gradient, owned):
    first_new = beta_one * first + (1.0 - beta_one) * gradient
    second_new = beta_two * second + (1.0 - beta_two) * gradient * gradient
    weight_new = weight - step_rate * first_new / (jnp.sqrt(second_new) + adam_floor)
    weight_new = jnp.where(owned, weight_new, 0.0).astype(bf16)
    return (weight_new[None], first_new[None], second_new[None])


def body(
    tokens,
    cotangent,
    value_weight,
    output_weight,
    value_first,
    output_first,
    value_second,
    output_second,
    layer_map,
    old_section,
    new_section,
):
    sections = lax.axis_size(section)
    width = lax.axis_size("z")
    myself = lax.axis_index(section)
    column = lax.axis_index("z")
    new = new_section.shape[0]
    features, channels = value_weight.shape[1:]
    part = features // sections
    positions = lax.iota(jnp.int32, sections)
    owner_match = positions[:, None] == new_section[None, :]
    map_match = layer_map[:, None] == lax.iota(jnp.int32, old_section.shape[0])[None, :]
    source = jnp.sum(jnp.where(map_match, old_section[None, :], 0), axis=1)
    holds = jnp.any(owner_match, axis=1)
    wanted = jnp.sum(jnp.where(owner_match, source[None, :], 0), axis=1)
    owned = jnp.any(new_section == myself)
    my_layer = jnp.sum(jnp.where(new_section == myself, lax.iota(jnp.int32, new), 0))
    my_old = jnp.sum(jnp.where(lax.iota(jnp.int32, new) == my_layer, layer_map, 0))

    def pieces_of(arrays):
        return jnp.stack([a.reshape(sections, part, channels).astype(bf16) for a in arrays], axis=1)

    def spread(a):
        return lax.all_to_all(a, section, split_axis=0, concat_axis=0, tiled=True)

    def turned(a):
        return a.reshape(2, ring, ring, part, channels).transpose(2, 1, 0, 3, 4)

    old = old_section.shape[0]
    pieces = spread(pieces_of((turned(value_weight), turned(output_weight))))
    deep = deep_of(2 * old)
    unit = jnp.minimum(
        groups * lax.iota(jnp.int32, deep)[None, :] + lax.iota(jnp.int32, groups)[:, None], 2 * old - 1
    ).reshape(-1)
    unit_match = (unit // 2)[:, None] == lax.iota(jnp.int32, old)[None, :]
    slots = 2 * jnp.sum(jnp.where(unit_match, old_section[None, :], 0), axis=1) + unit % 2
    count = tokens.shape[0] // sections

    def mine(a):
        block = lax.dynamic_slice_in_dim(a, myself * count, count, axis=0).astype(f32)
        return jnp.pad(block, ((0, rows - count), (0, 0)))

    numbers = lax.iota(jnp.int32, old)
    twice = (jnp.sum((layer_map[:, None] == numbers[None, :]).astype(jnp.int32), axis=0) > 1).astype(jnp.int32)
    before = jnp.concatenate([jnp.full((1,), -1, jnp.int32), layer_map[:-1]])
    place_of = 2 * layer_map + (before == layer_map).astype(jnp.int32)
    pieces, slots, twice, starting = lax.optimization_barrier((pieces, slots, twice, mine(tokens)))
    own = pick_slots(slots, jnp.ones_like(slots), pieces.reshape(2 * sections, part, channels))
    gathered, saved_in, hidden, pre, units = gather_forward(
        twice, own.reshape(groups, deep, part, channels), starting
    )
    gathered = gathered.reshape(groups, deep, sections, width, part, channels)
    moments = spread(pieces_of((value_first, output_first, value_second, output_second)))

    send_place = jnp.sum(jnp.where(owner_match, place_of[None, :], 0), axis=1)
    places = lax.iota(jnp.int32, 2 * old)
    send_layer = ((send_place[:, None] == places[None, :]) & holds[:, None]).astype(bf16)

    def message(choice, wide, narrow):
        w = pick(choice, wide)
        n = pick(choice, narrow)
        n = n.reshape(sections, rows, width, channels).transpose(0, 2, 1, 3)
        w = jnp.broadcast_to(w[:, None], (sections, width) + w.shape[1:])
        return [w, n]

    entering = mine(cotangent)
    moments, saved_in = lax.optimization_barrier((moments, saved_in))
    moments = pick_slots(wanted, holds.astype(jnp.int32), moments)
    moments, entering = lax.optimization_barrier((moments, entering))
    moments = spread(moments)
    grads, inner_grads = run_backward(new, twice, entering, gathered, saved_in, pre)
    sent = message(send_layer, hidden, units) + message(owner_match.astype(bf16), grads, inner_grads)
    sent = jnp.concatenate(sent, axis=-1)
    sent = sent.reshape((sections * width,) + sent.shape[2:])
    got = lax.all_to_all(sent, both, split_axis=0, concat_axis=0, tiled=True)
    got = got.reshape(sections * width * rows, got.shape[-1])
    fold = features // 2
    low = (lax.broadcasted_iota(jnp.int32, (got.shape[0], 1), 0) % rows) < rows // 2

    def weight_grad(a, b):
        b = jnp.concatenate([jnp.where(low, b, 0), jnp.where(low, 0, b)], axis=1)
        g = lax.dot_general(a, b, (((0,), (0,)), ((), ())), preferred_element_type=f32)
        return jnp.concatenate([g[:, :channels], g[:, channels:]], axis=0)

    grad_value = weight_grad(got[:, :fold], got[:, 2 * fold + channels :])
    grad_output = weight_grad(got[:, fold + channels : 2 * fold + channels], got[:, fold : fold + channels])

    def own_of(which):
        unit = 2 * my_old + which
        got = lax.dynamic_slice(
            gathered,
            (unit % groups, unit // groups, 0, column, 0, 0),
            (1, 1, sections, 1, part, channels),
        )
        return got.reshape(features, channels).astype(f32)

    moments = moments.astype(f32)

    def full(a):
        return a.reshape(features, channels)

    value_new = adam_update(own_of(0), full(moments[:, 0]), full(moments[:, 2]), grad_value, owned)
    output_new = adam_update(own_of(1), full(moments[:, 1]), full(moments[:, 3]), grad_output, owned)
    return (value_new[0], output_new[0], value_new[1], output_new[1], value_new[2], output_new[2])


def solution(mesh):
    split = P(section, None, "z")
    placed = (P("z", None),) * 2 + (split,) * 6 + (P(),) * 3
    fine = Mesh(mesh.devices.reshape(ring, ring, 2, ring), both)
    return jax.shard_map(body, mesh=fine, in_specs=placed, out_specs=(split,) * 6, check_vma=False)
```

```python
import jax
import jax.numpy as jnp
from jax import lax
from jax.experimental import pallas as pl
from jax.experimental.pallas import tpu as pltpu
from jax.sharding import Mesh
from jax.sharding import PartitionSpec as P

epsilon = 1e-05
beta_one = 0.9
beta_two = 0.95
step_rate = 0.003
adam_floor = 1e-08
f32 = jnp.float32
bf16 = jnp.bfloat16
section = ("y", "x", "c")
both = ("y", "x", "c", "z")
orders = (("x", "y", "z"), ("y", "z", "x"), ("z", "x", "y"))
ring = 4
groups = 3
rows = 8
ahead = 4
early = 3
MESH = pl.DeviceIdType.MESH


def deep_of(units):
    return -(-units // groups)


def folded(a):
    half = a.shape[1] // 2
    return (a[:, :half] + jnp.roll(a[:, half:], rows // 2, axis=0)).astype(bf16)


def repeated(a):
    return (a + jnp.roll(a, rows // 2, axis=0)).astype(bf16)


def forward_layer(x, value, output):
    factor = lax.rsqrt(jnp.mean(x * x, axis=-1, keepdims=True) + epsilon)
    hidden = (x * factor).astype(bf16)
    pre = jnp.dot(hidden, value, preferred_element_type=f32)
    units = jax.nn.silu(pre).astype(bf16)
    mixing = lax.dot_general(units, output, (((1,), (1,)), ((), ())), preferred_element_type=f32)
    return (x + mixing).astype(bf16).astype(f32), hidden, pre, units


def gather_kernel(
    old,
    twice_ref,
    own_ref,
    x_ref,
    out_ref,
    in_ref,
    hid_ref,
    pre_ref,
    unit_ref,
    held,
    state,
    send_one,
    recv_one,
    send,
    recv,
    load_sem,
    own_sem,
):
    deep = deep_of(2 * old)
    me = {a: lax.axis_index(a) for a in both}

    def beside(axis, step):
        size = 2 if axis == "c" else ring
        return {axis: lax.rem(me[axis] + step + size, size)}

    barrier = pltpu.get_barrier_semaphore()
    partners = [beside(a, s) for a in ("x", "y", "z") for s in (1, -1)] + [beside("c", 1)]
    for p in partners:
        pl.semaphore_signal(barrier, inc=1, device_id=p, device_id_type=MESH)
    pl.semaphore_wait(barrier, len(partners))

    def copy(src, dst, to, send_sem, recv_sem):
        return pltpu.make_async_remote_copy(
            src_ref=src,
            dst_ref=dst,
            send_sem=send_sem,
            recv_sem=recv_sem,
            device_id=to,
            device_id_type=MESH,
        )

    def place(g, phase, k, at, half):
        full = orders[g][:phase]
        axis = orders[g][phase]
        index = dict(me)
        for a in full:
            index[a] = pl.ds(0, ring)
        if half is not None and full:
            index[full[0]] = pl.ds(half * (ring // 2), ring // 2)
        index[axis] = at
        return out_ref.at[g, k, me["c"], index["x"], index["y"], index["z"]]

    spans = ((0, early), (early, deep - early))

    def bulk_first(g, b):
        axis = orders[g][0]
        part = pl.ds(*spans[b])
        dst = place(g, 0, part, me[axis], None)
        return [
            copy(own_ref.at[g, part], dst, beside(axis, s), send_one.at[g, n], recv_one.at[g, n])
            for n, s in ((4 * b, 1), (4 * b + 1, -1))
        ]

    def bulk_second(g, b):
        axis = orders[g][0]
        lo, size = spans[b]
        cut = size // 2
        out = []
        for n, s, lo, size in ((4 * b + 2, 1, lo, cut), (4 * b + 3, -1, lo + cut, size - cut)):
            part = place(g, 0, pl.ds(lo, size), lax.rem(me[axis] - s + ring, ring), None)
            out.append(copy(part, part, beside(axis, s), send_one.at[g, n], recv_one.at[g, n]))
        return out

    def first(g, phase, k):
        axis = orders[g][phase]
        here = place(g, phase, k, me[axis], None)
        base = 4 * (phase - 1)
        return [
            copy(here, here, beside(axis, s), send.at[g, k, base + n], recv.at[g, k, base + n])
            for n, s in ((0, 1), (1, -1))
        ]

    def second(g, phase, k):
        axis = orders[g][phase]
        base = 4 * (phase - 1) + 2
        out = []
        for n, s in ((0, 1), (1, -1)):
            part = place(g, phase, k, lax.rem(me[axis] - s + ring, ring), n)
            out.append(copy(part, part, beside(axis, s), send.at[g, k, base + n], recv.at[g, k, base + n]))
        return out

    def cross(g, k):
        block = out_ref.at[g, k, me["c"]]
        return [copy(block, block, beside("c", 1), send.at[g, k, 8], recv.at[g, k, 8])]

    def start(copies):
        for c in copies:
            c.start()

    def arrived(copies):
        for c in copies:
            c.wait_recv()

    def each(k, before, after, *more):
        for g in range(groups):
            if before is not None:
                arrived(before(g, *more, k))
            start(after(g, *more, k))

    def spread_start(k):
        each(k, None, lambda g, k: first(g, 1, k))

    def spread_pass(k):
        each(k, lambda g, k: first(g, 1, k), lambda g, k: second(g, 1, k))

    def plane_start(k):
        each(k, lambda g, k: second(g, 1, k), lambda g, k: first(g, 2, k))

    def plane_pass(k):
        each(k, lambda g, k: first(g, 2, k), lambda g, k: second(g, 2, k))

    def cross_start(k):
        each(k, lambda g, k: second(g, 2, k), cross)

    def load(g, k):
        unit = groups * k + g
        layer = lax.div(unit, 2)
        return pltpu.make_async_copy(
            out_ref.at[g, k], held.at[lax.rem(layer, 2), lax.rem(unit, 2)], load_sem.at[g]
        )

    def evaluate(q, carry):
        layer = lax.div(q, 2)
        again = lax.rem(q, 2)
        slot = lax.rem(layer, 2)
        x = state[...]
        following, hidden, pre, units = forward_layer(x, wide(held[slot, 0]), wide(held[slot, 1]))
        in_ref[q] = x.astype(bf16)
        hid_ref[q] = folded(hidden.astype(f32))
        pre_ref[q] = pre
        unit_ref[q] = repeated(units.astype(f32))
        keep = jnp.maximum(twice_ref[layer], 1 - again) > 0
        state[...] = jnp.where(keep, following, x)
        return carry

    def use(k):
        for g in range(groups):
            arrived(cross(g, k))
            load(g, k).start()
        for g in range(groups):
            load(g, k).wait()
        done = jnp.minimum(lax.div(groups * k + groups, 2), old)
        lax.fori_loop(2 * lax.div(groups * k, 2), 2 * done, evaluate, 0)

    mine = pltpu.make_async_copy(
        own_ref, out_ref.at[:, :, me["c"], me["x"], me["y"], me["z"]], own_sem
    )
    mine.start()
    for b in range(2):
        for g in range(groups):
            start(bulk_first(g, b))
    state[...] = x_ref[...]

    def bulk_pass(b):
        for g in range(groups):
            arrived(bulk_first(g, b))
            start(bulk_second(g, b))

    def bulk_end(b):
        for g in range(groups):
            arrived(bulk_second(g, b))

    bulk_pass(0)
    mine.wait()
    bulk_end(0)
    for k in range(early):
        spread_start(k)
    bulk_pass(1)
    spread_pass(0)
    spread_pass(1)
    plane_start(0)
    bulk_end(1)
    spread_pass(2)
    spread_start(3)
    plane_start(1)

    def drain(k):
        for g in range(groups):
            for phase in (1, 2):
                for c in first(g, phase, k) + second(g, phase, k):
                    c.wait_send()
            for c in cross(g, k):
                c.wait_send()

    def step(t, carry):
        def at(k, act):
            @pl.when((k >= 0) & (k < deep))
            def _():
                act(k)

        at(t - 1, cross_start)
        at(t, plane_pass)
        at(t + 2, plane_start)
        at(t + 3, spread_pass)
        at(t + 4, spread_start)
        at(t - 2, use)
        at(t - 3, drain)

        @pl.when(t == 1)
        def _():
            for g in range(groups):
                for b in range(2):
                    for c in bulk_first(g, b) + bulk_second(g, b):
                        c.wait_send()

        return carry

    lax.fori_loop(0, deep + 2, step, 0)
    drain(deep - 1)


def gather_forward(twice, own, x):
    old = twice.shape[0]
    deep, part, channels = own.shape[-3:]
    features = x.shape[1]
    inner = ring * channels
    shape = jax.ShapeDtypeStruct
    vmem = pl.BlockSpec(memory_space=pltpu.VMEM)
    hbm = pl.BlockSpec(memory_space=pl.ANY)
    unit = (2, ring, ring, ring, part, channels)
    return pl.pallas_call(
        lambda *refs: gather_kernel(old, *refs),
        in_specs=[pl.BlockSpec(memory_space=pltpu.SMEM), hbm, vmem],
        out_specs=[hbm, vmem, vmem, vmem, vmem],
        out_shape=[
            shape(own.shape[:2] + unit, bf16),
            shape((2 * old, rows, features), bf16),
            shape((2 * old, rows, features // 2), bf16),
            shape((2 * old, rows, inner), f32),
            shape((2 * old, rows, inner), bf16),
        ],
        scratch_shapes=[
            pltpu.VMEM((2, 2) + unit, bf16),
            pltpu.VMEM(x.shape, f32),
            pltpu.SemaphoreType.DMA((groups, 8)),
            pltpu.SemaphoreType.DMA((groups, 8)),
            pltpu.SemaphoreType.DMA((groups, deep, 9)),
            pltpu.SemaphoreType.DMA((groups, deep, 9)),
            pltpu.SemaphoreType.DMA((groups,)),
            pltpu.SemaphoreType.DMA,
        ],
        compiler_params=pltpu.CompilerParams(
            collective_id=0, has_side_effects=True, vmem_limit_bytes=48 * 2**20
        ),
        cost_estimate=pl.CostEstimate(
            flops=2 * old * rows * 8 * features * inner // 2,
            bytes_accessed=400 * 2**20,
            transcendentals=0,
        ),
    )(twice, own, x)


def wide(w):
    w = w.reshape((-1,) + w.shape[-3:])
    return jnp.concatenate([w[:, z].reshape(-1, w.shape[-1]) for z in range(w.shape[1])], axis=1)


def backward_layer(x, pre, g, value, output):
    gb = g.astype(bf16)
    gu = jnp.dot(gb, output, preferred_element_type=f32)
    s = jax.nn.sigmoid(pre)
    gz = (gu * s * (1.0 + pre * (1.0 - s))).astype(bf16)
    gh = lax.dot_general(gz, value, (((1,), (1,)), ((), ())), preferred_element_type=f32)
    factor = lax.rsqrt(jnp.mean(x * x, axis=-1, keepdims=True) + epsilon)
    n = x * factor
    gs = factor * (gh - n * jnp.mean(gh * n, axis=-1, keepdims=True))
    return (g + gs).astype(bf16).astype(f32), gb, gz


def backward_kernel(
    twice_ref, g_ref, weight_ref, in_ref, pre_ref, out_g_ref, out_z_ref, held, state, load_sem
):
    old = in_ref.shape[0] // 2
    new = out_g_ref.shape[0]

    def loads(n):
        out = []
        for h in range(2):
            unit = 2 * (old - 1 - n) + h
            slot = lax.rem(n, ahead)
            src = weight_ref.at[lax.rem(unit, groups), lax.div(unit, groups)]
            out.append(pltpu.make_async_copy(src, held.at[slot, h], load_sem.at[slot, h]))
        return out

    def start(n):
        for c in loads(n):
            c.start()

    for n in range(ahead):
        start(n)
    state[...] = g_ref[...]

    def layer(n, j):
        for c in loads(n):
            c.wait()
        slot = lax.rem(n, ahead)
        i = old - 1 - n
        extra = twice_ref[i]

        def evaluate(r, j):
            q = 2 * i + extra - r
            x = in_ref[q].astype(f32)
            g, gb, gz = backward_layer(x, pre_ref[q], state[...], wide(held[slot, 0]), wide(held[slot, 1]))
            out_g_ref[j] = folded(gb.astype(f32))
            out_z_ref[j] = repeated(gz.astype(f32))
            state[...] = g
            return j - 1

        j = lax.fori_loop(0, extra + 1, evaluate, j)

        @pl.when(n + ahead < old)
        def _():
            start(n + ahead)

        return j

    lax.fori_loop(0, old, layer, new - 1)


def run_backward(new, twice, g, weights, saved_in, pre):
    shape = jax.ShapeDtypeStruct
    vmem = pl.BlockSpec(memory_space=pltpu.VMEM)
    size = 2 * weights.size // (weights.shape[0] * weights.shape[1]) * 2 * twice.shape[0]
    return pl.pallas_call(
        backward_kernel,
        in_specs=[
            pl.BlockSpec(memory_space=pltpu.SMEM),
            vmem,
            pl.BlockSpec(memory_space=pl.ANY),
            vmem,
            vmem,
        ],
        out_specs=[vmem, vmem],
        out_shape=[
            shape((new, rows, saved_in.shape[2] // 2), bf16),
            shape((new, rows, pre.shape[2]), bf16),
        ],
        scratch_shapes=[
            pltpu.VMEM((ahead, 2) + weights.shape[2:], bf16),
            pltpu.VMEM(g.shape, f32),
            pltpu.SemaphoreType.DMA((ahead, 2)),
        ],
        compiler_params=pltpu.CompilerParams(vmem_limit_bytes=48 * 2**20),
        cost_estimate=pl.CostEstimate(
            flops=2 * rows * size, bytes_accessed=2 * size, transcendentals=0
        ),
    )(twice, g, weights, saved_in, pre)


def pick_kernel(index_ref, keep_ref, in_ref, out_ref):
    def one(k, carry):
        kept = in_ref[index_ref[k]] * keep_ref[k].astype(f32).astype(bf16)
        out_ref[k] = kept
        return carry

    lax.fori_loop(0, out_ref.shape[0], one, 0)


def pick_slots(index, keep, pieces):
    whole = pl.BlockSpec(memory_space=pltpu.VMEM)
    scalar = pl.BlockSpec(memory_space=pltpu.SMEM)
    flat = pieces.reshape(pieces.shape[0], -1, pieces.shape[-1])
    got = pl.pallas_call(
        pick_kernel,
        in_specs=[scalar, scalar, whole],
        out_specs=whole,
        out_shape=jax.ShapeDtypeStruct((index.shape[0],) + flat.shape[1:], bf16),
        compiler_params=pltpu.CompilerParams(vmem_limit_bytes=24 * 2**20),
    )(index, keep, flat)
    return got.reshape((index.shape[0],) + pieces.shape[1:])


def pick(onehot, pieces):
    flat = pieces.reshape(pieces.shape[0], -1, pieces.shape[-1])
    got = lax.dot_general(onehot, flat, (((1,), (0,)), ((), ())), preferred_element_type=bf16)
    return got.reshape((onehot.shape[0],) + pieces.shape[1:])


def adam_update(weight, first, second, gradient, owned):
    first_new = beta_one * first + (1.0 - beta_one) * gradient
    second_new = beta_two * second + (1.0 - beta_two) * gradient * gradient
    weight_new = weight - step_rate * first_new / (jnp.sqrt(second_new) + adam_floor)
    weight_new = jnp.where(owned, weight_new, 0.0).astype(bf16)
    return (weight_new[None], first_new[None], second_new[None])


def body(
    tokens,
    cotangent,
    value_weight,
    output_weight,
    value_first,
    output_first,
    value_second,
    output_second,
    layer_map,
    old_section,
    new_section,
):
    sections = lax.axis_size(section)
    width = lax.axis_size("z")
    myself = lax.axis_index(section)
    column = lax.axis_index("z")
    new = new_section.shape[0]
    features, channels = value_weight.shape[1:]
    part = features // sections
    positions = lax.iota(jnp.int32, sections)
    owner_match = positions[:, None] == new_section[None, :]
    map_match = layer_map[:, None] == lax.iota(jnp.int32, old_section.shape[0])[None, :]
    source = jnp.sum(jnp.where(map_match, old_section[None, :], 0), axis=1)
    holds = jnp.any(owner_match, axis=1)
    wanted = jnp.sum(jnp.where(owner_match, source[None, :], 0), axis=1)
    owned = jnp.any(new_section == myself)
    my_layer = jnp.sum(jnp.where(new_section == myself, lax.iota(jnp.int32, new), 0))
    my_old = jnp.sum(jnp.where(lax.iota(jnp.int32, new) == my_layer, layer_map, 0))

    def pieces_of(arrays):
        return jnp.stack([a.reshape(sections, part, channels).astype(bf16) for a in arrays], axis=1)

    def spread(a):
        return lax.all_to_all(a, section, split_axis=0, concat_axis=0, tiled=True)

    def turned(a):
        return a.reshape(2, ring, ring, part, channels).transpose(2, 1, 0, 3, 4)

    old = old_section.shape[0]
    pieces = spread(pieces_of((turned(value_weight), turned(output_weight))))
    deep = deep_of(2 * old)
    unit = jnp.minimum(
        groups * lax.iota(jnp.int32, deep)[None, :] + lax.iota(jnp.int32, groups)[:, None], 2 * old - 1
    ).reshape(-1)
    unit_match = (unit // 2)[:, None] == lax.iota(jnp.int32, old)[None, :]
    slots = 2 * jnp.sum(jnp.where(unit_match, old_section[None, :], 0), axis=1) + unit % 2
    count = tokens.shape[0] // sections

    def mine(a):
        block = lax.dynamic_slice_in_dim(a, myself * count, count, axis=0).astype(f32)
        return jnp.pad(block, ((0, rows - count), (0, 0)))

    numbers = lax.iota(jnp.int32, old)
    twice = (jnp.sum((layer_map[:, None] == numbers[None, :]).astype(jnp.int32), axis=0) > 1).astype(jnp.int32)
    before = jnp.concatenate([jnp.full((1,), -1, jnp.int32), layer_map[:-1]])
    place_of = 2 * layer_map + (before == layer_map).astype(jnp.int32)
    pieces, slots, twice, starting = lax.optimization_barrier((pieces, slots, twice, mine(tokens)))
    own = pick_slots(slots, jnp.ones_like(slots), pieces.reshape(2 * sections, part, channels))
    gathered, saved_in, hidden, pre, units = gather_forward(
        twice, own.reshape(groups, deep, part, channels), starting
    )
    gathered = gathered.reshape(groups, deep, sections, width, part, channels)
    moments = spread(pieces_of((value_first, output_first, value_second, output_second)))

    send_place = jnp.sum(jnp.where(owner_match, place_of[None, :], 0), axis=1)
    places = lax.iota(jnp.int32, 2 * old)
    send_layer = ((send_place[:, None] == places[None, :]) & holds[:, None]).astype(bf16)

    def message(choice, wide, narrow):
        w = pick(choice, wide)
        n = pick(choice, narrow)
        n = n.reshape(sections, rows, width, channels).transpose(0, 2, 1, 3)
        w = jnp.broadcast_to(w[:, None], (sections, width) + w.shape[1:])
        return [w, n]

    entering = mine(cotangent)
    moments, saved_in = lax.optimization_barrier((moments, saved_in))
    moments = pick_slots(wanted, holds.astype(jnp.int32), moments)
    moments, entering = lax.optimization_barrier((moments, entering))
    moments = spread(moments)
    grads, inner_grads = run_backward(new, twice, entering, gathered, saved_in, pre)
    sent = message(send_layer, hidden, units) + message(owner_match.astype(bf16), grads, inner_grads)
    sent = jnp.concatenate(sent, axis=-1)
    sent = sent.reshape((sections * width,) + sent.shape[2:])
    got = lax.all_to_all(sent, both, split_axis=0, concat_axis=0, tiled=True)
    got = got.reshape(sections * width * rows, got.shape[-1])
    fold = features // 2
    low = (lax.broadcasted_iota(jnp.int32, (got.shape[0], 1), 0) % rows) < rows // 2

    def weight_grad(a, b):
        b = jnp.concatenate([jnp.where(low, b, 0), jnp.where(low, 0, b)], axis=1)
        g = lax.dot_general(a, b, (((0,), (0,)), ((), ())), preferred_element_type=f32)
        return jnp.concatenate([g[:, :channels], g[:, channels:]], axis=0)

    grad_value = weight_grad(got[:, :fold], got[:, 2 * fold + channels :])
    grad_output = weight_grad(got[:, fold + channels : 2 * fold + channels], got[:, fold : fold + channels])

    def own_of(which):
        unit = 2 * my_old + which
        got = lax.dynamic_slice(
            gathered,
            (unit % groups, unit // groups, 0, column, 0, 0),
            (1, 1, sections, 1, part, channels),
        )
        return got.reshape(features, channels).astype(f32)

    moments = moments.astype(f32)

    def full(a):
        return a.reshape(features, channels)

    value_new = adam_update(own_of(0), full(moments[:, 0]), full(moments[:, 2]), grad_value, owned)
    output_new = adam_update(own_of(1), full(moments[:, 1]), full(moments[:, 3]), grad_output, owned)
    return (value_new[0], output_new[0], value_new[1], output_new[1], value_new[2], output_new[2])


def solution(mesh):
    split = P(section, None, "z")
    placed = (P("z", None),) * 2 + (split,) * 6 + (P(),) * 3
    fine = Mesh(mesh.devices.reshape(ring, ring, 2, ring), both)
    return jax.shard_map(body, mesh=fine, in_specs=placed, out_specs=(split,) * 6, check_vma=False)
```
